512 devices in a mesh: ctx: 32 (over y, x), tp: 16 (over z, core).
Axes of the slice: x: 4, y: 8, z: 8, core: 2. Of those that a mesh axis runs over, the one named last changes fastest.
Arguments:
- queries: bfloat16 [2048, 4096], P('ctx', 'tp'), may hold values from -6 to 6
- key_rows: bfloat16 [2048, 4096], P('ctx', 'tp'), may hold values from -6 to 6
- value_rows: bfloat16 [2048, 4096], P('ctx', 'tp'), may hold values from -6 to 6
- out_gate: bfloat16 [2048, 4096], P('ctx', 'tp'), may hold values from -9.5 to 6.5
- decay_index: int32 [32], P('tp'), may hold values from 0 to 15
- w_out: bfloat16 [4096, 3072], P('tp'), may hold values from -1 to 1
- norm_gain: float32 [3072], replicated, may hold values from 0.5 to 1.5
- expert_ids: int32 [2048, 2], P('ctx'), may hold values from 0 to 15, all different within a row; in each aligned block of 64 rows (0 to 63, 64 to 127, ...) at most 9 rows name the same one
- gate_codes: int32 [2048, 2], P('ctx'), may hold values from 1 to 1023
- w_gate: bfloat16 [32, 3072, 2304], P('ctx', None, 'tp'), may hold values from -0.109375 to 0.109375
- w_up: bfloat16 [32, 3072, 2304], P('ctx', None, 'tp'), may hold values from -0.109375 to 0.109375
- w_down: bfloat16 [32, 2304, 3072], P('ctx', 'tp'), may hold values from -0.125 to 0.125
Outputs:
- mixed: bfloat16 [2048, 3072], P('ctx', 'tp')
The draws below stay inside these ranges and needn't reach their ends.
Inputs may be any that keep to these rules, and one draw needn't show every extreme that they name: `expert_ids`: the 2 ids of a token differ. Within the tokens of one index of ctx (aligned blocks of 64 tokens) each expert is named by at most 9 tokens, a bound that some block reaches.
All inputs are finite; a program needn't handle non-finite values.
Results may differ from the reference program's by a relative error of at most 0.015.
Values may be sent and summed in bfloat16 or wider, within the bound.
A program may use at most 64 MiB of HBM per device.

```python
import math
import jax
import jax.numpy as jnp
import numpy as np
from jax import lax

HEADS = 32
HEAD = 128
D = 3072
FF = 4608
EXPERTS = 16
TOP = 2
NLEV = 16
TOK_CTX = 64
CAP = 9
TOKENS = 2048
GROUP_UNITS = 144
N_CTX = 32


def draw_out_gate(key, part):
    first_key, second_key = jax.random.split(key, 2)
    jitter = jnp.clip(jax.random.normal(first_key, (TOKENS, HEADS * HEAD), jnp.float32), -3.0, 3.0)
    offset = jax.random.uniform(second_key, (TOKENS, 1), jnp.float32, -4.0, 1.5)
    values = offset + jitter
    return values.astype(jnp.bfloat16)


def draw_w_out(key, part):
    first_key, second_key = jax.random.split(key, 2)
    fan_rows = HEADS * HEAD
    normal_part = jnp.clip(jax.random.normal(first_key, (fan_rows, D), jnp.float32), -5.0, 5.0)
    columns = jnp.arange(D, dtype=jnp.float32) / (D - 1.0)
    levels = jax.random.uniform(second_key, (D,), jnp.float32, 0.0, 1.0)
    ramps = 3.0 ** (0.5 * columns)
    scales = 10.0 ** levels * ramps
    scales = scales / jnp.sqrt(jnp.mean(scales * scales))
    values = normal_part * scales[None, :] / jnp.sqrt(fan_rows * 1.0)
    return jnp.clip(values, -1.0, 1.0).astype(jnp.bfloat16)


def touch_ends(entries, own_key, least, largest):
    extent = entries.shape
    index_at = [jax.random.randint(jax.random.fold_in(own_key, axis), (), 0, extent[axis]) for axis in range(len(extent))]
    entries = entries.at[tuple(index_at)].set(least)
    longest = extent.index(max(extent))
    index_at[longest] = (index_at[longest] + 1) % extent[longest]
    return entries.at[tuple(index_at)].set(largest)


def with_spikes(result, own_key, source, target, parts, factor):
    def block_of(dim):
        return (jnp.arange(result.shape[dim]) // (result.shape[dim] // parts)).reshape((-1,) + (1,) * (result.ndim - 1 - dim))

    near = jax.random.permutation(own_key, parts)[block_of(target)]
    other_side = (block_of(target) + parts // 2) % parts
    return jnp.where((block_of(source) == near) | (block_of(source) == other_side), factor * result, result)


def level_of(key, dims, cuts, least, top_value):
    def one(dim, parts):
        heights = jax.random.uniform(jax.random.fold_in(jax.random.fold_in(key, 6), dim), (parts,), jnp.float32, least / len(cuts), top_value / len(cuts))
        return jnp.repeat(jnp.exp(heights), dims[dim] // parts).reshape((-1,) + (1,) * (len(dims) - dim - 1))

    level = one(*cuts[0])
    for cut in cuts[1:]:
        level = level * one(*cut)
    return level


def routed_block(key, own, number, rows, amount, top, most, skew):
    sequence = jax.random.permutation(key, amount)
    crowded, usual = portions_of(amount, rows * top, most, skew, True), portions_of(amount, rows * top, most, skew, False)
    places = jnp.arange(amount)

    def named(sizes, turn):
        used = int((sizes > 0).sum())
        fixed = max(1, used // 4)
        moved = fixed + (places - fixed + turn * (used - fixed)) % max(1, amount - fixed)
        return jnp.zeros((amount,), jnp.int32).at[sequence[jnp.where(places < fixed, places, moved)]].set(jnp.asarray(sizes, jnp.int32))

    sizes = jnp.where(number % 4 == 0, named(crowded, number // 4), named(usual, number - number // 4 - 1))
    mixed = jax.random.permutation(jax.random.fold_in(own, 3), amount)
    giver, taker = mixed[0:amount // 2 * 2:2], mixed[1:amount // 2 * 2:2]
    margin = jnp.minimum(sizes[giver] - 1, most - sizes[taker]) // 2
    margin = jnp.where((giver == sequence[0]) | (taker == sequence[0]) | (sizes[taker] == 0), 0, jnp.maximum(margin, 0))
    moved = jax.random.randint(jax.random.fold_in(own, 4), (amount // 2,), 0, 1 << 20) % (margin + 1)
    sizes = sizes.at[giver].add(-moved).at[taker].add(moved)
    labels = jnp.searchsorted(jnp.cumsum(sizes), jnp.arange(rows * top), side="right").astype(jnp.int32)
    listing = labels.reshape(top, rows).T
    listing = listing[jax.random.permutation(jax.random.fold_in(own, 1), rows)]
    turn = jax.random.randint(jax.random.fold_in(own, 2), (rows, 1), 0, top)
    return jnp.take_along_axis(listing, (jnp.arange(top)[None, :] + turn) % top, axis=1)


def portions_of(count, total, reach, lean, full):
    loads = [(1 << 20) // math.isqrt(grade ** lean) + 1 for grade in range(1, count + 1)]
    largest = reach if full else min(reach, max(-(-total // count), total * loads[0] // sum(loads)))
    least = 1 if total - largest >= count - 1 else 0
    given, rest = [largest] + [least] * (count - 1), total - largest - least * (count - 1)
    while rest > 0:
        candidates = [i for i in range(1, count) if given[i] < largest] or [i for i in range(1, count) if given[i] < reach]
        pool, left = sum([loads[i] for i in candidates]), rest
        for i in candidates:
            addition = min(reach - given[i], max(1, left * loads[i] // pool), rest)
            given[i] = given[i] + addition
            rest = rest - addition
    return np.array(given)


def bell_draw(stream_key, dims, scale, most, cuts=(), kind=jnp.bfloat16):
    gain = level_of(stream_key, dims, cuts, -0.22, 0.18) if cuts else 1.0
    entries = jax.random.normal(stream_key, dims, jnp.float32) * scale * gain
    return jnp.minimum(jnp.maximum(entries, -most), most).astype(kind)


def heavy_noise(own_key, extent, width, limit, cuts, heavy, held_as=jnp.bfloat16):
    values = width * jax.random.normal(own_key, extent, jnp.float32)
    if cuts:
        values = values * level_of(own_key, extent, cuts, -0.22, 0.18)
    return jnp.clip(with_spikes(values, jax.random.fold_in(own_key, 3), *heavy), -limit, limit).astype(held_as)


def setup_inputs(seed: int = 0) -> dict:
    seeds = jax.random.split(jax.random.key(seed), 13)
    queries = bell_draw(seeds[0], (TOKENS, HEADS * HEAD), 1.0, 6.0, ((0, 32), (1, 16)))
    key_rows = bell_draw(seeds[1], (TOKENS, HEADS * HEAD), 1.0, 6.0, ((0, 32), (1, 16)))
    value_rows = bell_draw(seeds[2], (TOKENS, HEADS * HEAD), 1.0, 6.0, ((0, 32), (1, 16)))
    out_gate = draw_out_gate(jax.random.fold_in(seeds[12], 71), 0)
    decay_index = touch_ends(jax.random.randint(seeds[4], (HEADS,), 0, NLEV), jax.random.fold_in(seeds[4], 1), 0, NLEV - 1).astype(jnp.int32)
    w_out = draw_w_out(jax.random.fold_in(seeds[12], 71), 0)
    norm_gain = jnp.clip(1.0 + 0.1 * jax.random.normal(seeds[6], (D,), jnp.float32), 0.5, 1.5)
    expert_ids_keys = jax.random.split(jax.random.fold_in(seeds[7], 1), TOKENS // TOK_CTX)
    expert_ids_turns = jax.random.permutation(jax.random.fold_in(seeds[7], 3), TOKENS // TOK_CTX)
    expert_ids = jax.vmap(lambda own, number: routed_block(jax.random.fold_in(seeds[7], 2), own, number, TOK_CTX, EXPERTS, TOP, CAP, 1))(expert_ids_keys, expert_ids_turns).reshape((TOKENS, TOP))
    gate_codes = touch_ends(jax.random.randint(seeds[8], (TOKENS, TOP), 1, 1024), jax.random.fold_in(seeds[8], 1), 1, 1023).astype(jnp.int32)
    w_gate = bell_draw(seeds[9], (2 * EXPERTS, D, FF // 2), D ** -0.5, 0.109375, ((0, 32), (2, 16)))
    w_up = bell_draw(seeds[10], (2 * EXPERTS, D, FF // 2), D ** -0.5, 0.109375, ((0, 32), (2, 16)))
    w_down = heavy_noise(seeds[11], (2 * EXPERTS, FF // 2, D), FF ** -0.5, 0.125, ((0, 32), (1, 16)), (1, 2, 16, 2.0))
    return dict(queries=queries, key_rows=key_rows, value_rows=value_rows, out_gate=out_gate, decay_index=decay_index, w_out=w_out, norm_gain=norm_gain, expert_ids=expert_ids, gate_codes=gate_codes, w_gate=w_gate, w_up=w_up, w_down=w_down)


def decay_rates(decay_index, seq_len):
    fraction = decay_index.astype(jnp.float32) / (NLEV - 1)
    fastest = jnp.log(jnp.float32(1.0 / 40.0))
    slowest = jnp.log(jnp.float32(1.0 / (16.0 * seq_len)))
    return jnp.exp(fastest + fraction * (slowest - fastest))

def head_attention(operands):
    query_part, key_part, value_part, decay_rate = operands
    places = jnp.arange(TOK_CTX, dtype=jnp.float32)
    offsets = places[:, None] - places[None, :]
    within = jnp.where(offsets >= 0.0, jnp.exp(-decay_rate * jnp.maximum(offsets, 0.0)), 0.0)
    entering = jnp.exp(-decay_rate * (places + 1.0))
    fading = jnp.exp(-decay_rate * (TOK_CTX - 1.0 - places))
    block_decay = jnp.exp(-decay_rate * TOK_CTX)

    def advance(carried, pieces):
        query_block, key_block, value_block = pieces
        attention_scores = jnp.dot(query_block, key_block.T, preferred_element_type=jnp.float32)
        routing_weights = (attention_scores * within).astype(jnp.bfloat16)
        intra_block_part = jnp.dot(routing_weights, value_block, preferred_element_type=jnp.float32)
        outside = jnp.dot(query_block.astype(jnp.float32), carried, precision=lax.Precision.HIGHEST) * entering[:, None]
        local_state = jnp.dot((key_block.astype(jnp.float32) * fading[:, None]).T, value_block.astype(jnp.float32), precision=lax.Precision.HIGHEST)
        return (block_decay * carried + local_state, intra_block_part + outside)
    _, attended = lax.scan(advance, jnp.zeros((HEAD, HEAD), jnp.float32), (query_part, key_part, value_part))
    return attended

def expert_apply(operands):
    expert_rows, gate_halves, up_halves, down_halves = operands
    gate_full = jnp.concatenate([gate_halves[0], gate_halves[1]], axis=1).astype(jnp.float32)
    up_full = jnp.concatenate([up_halves[0], up_halves[1]], axis=1).astype(jnp.float32)
    down_full = jnp.concatenate([down_halves[0], down_halves[1]], axis=0).astype(jnp.float32)
    rows_wide = expert_rows.astype(jnp.float32)
    gate_sum = jnp.dot(rows_wide, gate_full, preferred_element_type=jnp.float32)
    up_sum = jnp.dot(rows_wide, up_full, preferred_element_type=jnp.float32)
    hidden = lax.optimization_barrier((jax.nn.silu(gate_sum) * up_sum).astype(jnp.bfloat16))
    groups = FF // GROUP_UNITS
    group_parts = jnp.einsum('rgu,gud->rgd', hidden.reshape(-1, groups, GROUP_UNITS).astype(jnp.float32), down_full.reshape(groups, GROUP_UNITS, D))
    group_parts = lax.optimization_barrier(group_parts.astype(jnp.bfloat16))
    return lax.optimization_barrier(jnp.sum(group_parts.astype(jnp.float32), axis=1))

def reference(queries, key_rows, value_rows, out_gate, decay_index, w_out, norm_gain, expert_ids, gate_codes, w_gate, w_up, w_down):
    decays = decay_rates(decay_index, TOKENS)

    def split_heads(array):
        return array.reshape(N_CTX, TOK_CTX, HEADS, HEAD).transpose(2, 0, 1, 3)
    attended = lax.map(head_attention, (split_heads(queries), split_heads(key_rows), split_heads(value_rows), decays))
    attended = attended.transpose(1, 2, 0, 3).reshape(TOKENS, HEADS, HEAD)
    inverse_scale = lax.rsqrt(lax.optimization_barrier(jnp.mean(attended * attended, axis=2, keepdims=True)) + 1e-06)
    opening = jax.nn.sigmoid(out_gate.astype(jnp.float32)).reshape(TOKENS, HEADS, HEAD)
    heads_out = (attended * inverse_scale * opening).reshape(TOKENS, HEADS * HEAD).astype(jnp.bfloat16)
    summed = jnp.dot(heads_out, w_out, preferred_element_type=jnp.float32)
    row_inverse = lax.rsqrt(lax.optimization_barrier(jnp.mean(summed * summed, axis=1, keepdims=True)) + 1e-05)
    outgoing = (summed * row_inverse * norm_gain[None, :]).astype(jnp.bfloat16)
    blocks = expert_ids.reshape(N_CTX, TOP * TOK_CTX)
    indicator = (blocks[:, :, None] == jnp.arange(EXPERTS, dtype=jnp.int32)[None, None, :]).astype(jnp.int32)
    ranking = lax.optimization_barrier(jnp.sum((jnp.cumsum(indicator, axis=1) - indicator) * indicator, axis=2)).astype(jnp.int32)
    token_of = (jnp.arange(TOP * TOK_CTX, dtype=jnp.int32) // TOP).astype(jnp.int32)
    block_index = jnp.arange(N_CTX, dtype=jnp.int32)
    rows_of = outgoing.reshape(N_CTX, TOK_CTX, D)[block_index[:, None], token_of[None, :]]
    buffer = jnp.zeros((EXPERTS, N_CTX, CAP, D), jnp.bfloat16).at[blocks, block_index[:, None], ranking].set(rows_of)
    gate_pairs = w_gate.reshape(EXPERTS, 2, D, FF // 2)
    up_pairs = w_up.reshape(EXPERTS, 2, D, FF // 2)
    down_pairs = w_down.reshape(EXPERTS, 2, FF // 2, D)
    results = lax.map(expert_apply, (buffer.reshape(EXPERTS, N_CTX * CAP, D), gate_pairs, up_pairs, down_pairs))
    results = results.reshape(EXPERTS, N_CTX, CAP, D)
    routed = results[blocks, block_index[:, None], ranking]
    code_values = gate_codes.astype(jnp.float32)
    shares = (code_values / lax.optimization_barrier(jnp.sum(code_values, axis=1, keepdims=True))).reshape(N_CTX, TOP * TOK_CTX)
    moe = lax.optimization_barrier(jnp.sum((routed * shares[:, :, None]).reshape(TOKENS, TOP, D), axis=1))
    return (summed + moe).astype(jnp.bfloat16)
```

```python
import functools

import jax
import jax.numpy as jnp
from jax import lax
from jax.experimental import pallas as pl
from jax.experimental.pallas import tpu as pltpu
from jax.sharding import PartitionSpec as P

HEAD = 128
TOP = 2
NLEV = 16
CAP = 9
TOK = 64
HALF = TOK // 2
SLAB = 384
LANE = 128
TILES = SLAB // LANE
MSG = 32
UNITS = 144
MESH = pl.DeviceIdType.MESH
BF = jnp.bfloat16
F32 = jnp.float32


def mm(a, b):
    return jnp.dot(a, b, preferred_element_type=F32)


def mm_t(a, b):
    return lax.dot_general(a, b, (((0,), (0,)), ((), ())), preferred_element_type=F32)


def wait_bytes(ref, sem):
    pltpu.make_async_copy(ref, ref, sem).wait()


def iota(shape, dim):
    return lax.broadcasted_iota(jnp.int32, shape, dim)


def kernel(
    C,
    NT,
    TOKENS,
    idx_ref,
    q_ref,
    k_ref,
    v_ref,
    og_ref,
    gain_ref,
    ids_ref,
    codes_ref,
    wout_hbm,
    wg_hbm,
    wu_hbm,
    wd_hbm,
    out_ref,
    wout_v,
    wg_v,
    wu_v,
    wd_v,
    state_v,
    win_v,
    pst_v,
    prior_v,
    ho_v,
    hs_v,
    rst_v,
    rsb_v,
    pick_v,
    comb_v,
    res_v,
    mst_v,
    arr_v,
    x_v,
    sp_v,
    rp_v,
    m2_v,
    ret_v,
    fin_v,
    wl_sem,
    ws_sem,
    wr_sem,
    one_send,
    one_recv,
    ag_send,
    ag_recv,
    rs_send,
    rs_recv,
):
    NZ = NT // 2
    H = NZ // 2
    E = C // 2
    PR = 2 * HEAD // E
    RQ = x_v.shape[1]
    D = NZ * SLAB
    first = (RQ // 16 + 1) // 2 * 16
    parts = ((0, first), (first, RQ - first))

    c = lax.axis_index("ctx")
    t = lax.axis_index("tp")
    z = lax.div(t, 2)
    core = lax.rem(t, 2)
    sib = t + 1 - 2 * core
    side = lax.rem(c, 2)
    mine = lax.div(c, 2)
    active = side == core

    ST1, ST2, HO, RS, DISP, RETN, FIN = range(7)

    def put(src, dst, send, recv, ctx, tp):
        pltpu.make_async_remote_copy(
            src_ref=src,
            dst_ref=dst,
            send_sem=send,
            recv_sem=recv,
            device_id={"ctx": ctx, "tp": tp},
            device_id_type=MESH,
        ).start()

    barrier = pltpu.get_barrier_semaphore()

    def greet_ctx(i, carry):
        pl.semaphore_signal(
            barrier, inc=1, device_id={"ctx": lax.rem(c + i, C), "tp": t}, device_id_type=MESH
        )
        return carry

    def greet_tp(i, carry):
        pl.semaphore_signal(
            barrier, inc=1, device_id={"ctx": c, "tp": lax.rem(t + i, NT)}, device_id_type=MESH
        )
        return carry

    lax.fori_loop(1, C, greet_ctx, 0)
    lax.fori_loop(1, NT, greet_tp, 0)

    weights = (
        (wout_hbm, wout_v),
        (wg_hbm.at[0], wg_v),
        (wu_hbm.at[0], wu_v),
        (wd_hbm.at[0], wd_v),
    )
    for n, (src, dst) in enumerate(weights):
        pltpu.make_async_copy(src, dst.at[0], wl_sem.at[n]).start()

    log_fast = jnp.log(jnp.full((1, 1), 1.0 / 40.0, F32))
    log_slow = jnp.log(jnp.full((1, 1), 1.0 / (16.0 * TOKENS), F32))
    rates = []
    for h in range(2):
        fraction = jnp.full((1, 1), idx_ref[h].astype(F32), F32) / (NLEV - 1)
        rates.append(jnp.exp(log_fast + fraction * (log_slow - log_fast)))
    place = iota((TOK, 1), 0).astype(F32)
    for h in range(2):
        cols = slice(h * HEAD, (h + 1) * HEAD)
        fading = jnp.exp(-rates[h] * (TOK - 1.0 - place))
        faded = (k_ref[:, cols].astype(F32) * fading).astype(BF)
        state = mm_t(faded, v_ref[:, cols]).astype(BF)
        each = HEAD // PR
        state_v[h * each : (h + 1) * each] = state.reshape(each, PR, HEAD)

    pl.semaphore_wait(barrier, C - 1 + NT - 1)

    def send_piece(i, carry):
        j = lax.rem(mine + i, E)
        put(
            state_v.at[j], win_v.at[c], one_send.at[ST1], one_recv.at[ST1], 2 * j + core, t
        )
        return carry

    lax.fori_loop(1, E, send_piece, 0)

    @pl.when(jnp.logical_not(active))
    def _():
        send_piece(0, 0)

    for n, (src, dst) in enumerate(weights):
        put(src, dst.at[1], ws_sem.at[n], wr_sem.at[n], c, sib)

    n_at, m_at = iota((TOK, TOK), 0), iota((TOK, TOK), 1)
    offsets = (n_at - m_at).astype(F32)
    inside = []
    for h in range(2):
        cols = slice(h * HEAD, (h + 1) * HEAD)
        scores = lax.dot_general(
            q_ref[:, cols], k_ref[:, cols], (((1,), (1,)), ((), ())), preferred_element_type=F32
        )
        within = jnp.where(
            offsets >= 0.0, jnp.exp(-rates[h] * jnp.maximum(offsets, 0.0)), 0.0
        )
        inside.append(mm((scores * within).astype(BF), v_ref[:, cols]))

    @pl.when(active)
    def _():
        win_v[c] = state_v[mine]
        wait_bytes(win_v.at[pl.ds(0, C - 1)], one_recv.at[ST1])
        first_head = mine * PR < HEAD
        decay = jnp.exp(-jnp.where(first_head, rates[0], rates[1]) * TOK)

        def turn(b, run):
            pst_v[b] = run.astype(BF)
            return run * decay + win_v[b].astype(F32)

        lax.fori_loop(0, C, turn, jnp.zeros((PR, HEAD), F32), unroll=True)
        prior_v[mine] = pst_v[c]

        def send_prefix(i, carry):
            to = lax.rem(c + i, C)
            put(pst_v.at[to], prior_v.at[mine], one_send.at[ST2], one_recv.at[ST2], to, t)
            return carry

        lax.fori_loop(1, C, send_prefix, 0)

    @pl.when(active)
    def _():
        ids = ids_ref[...].astype(F32)
        codes = codes_ref[...].astype(F32)
        share = codes / jnp.sum(codes, axis=1, keepdims=True)
        expert_at = iota((TOK, LANE), 1).astype(F32)
        hot = [jnp.where(expert_at == ids[:, j : j + 1], 1.0, 0.0) for j in range(TOP)]
        before = jnp.where(n_at > m_at, 1.0, 0.0).astype(BF)
        count = mm(before, (hot[0] + hot[1]).astype(BF))
        rank = [jnp.sum(hot[j] * count, axis=1, keepdims=True) for j in range(TOP)]
        row_at = iota((TOK, E * MSG), 1).astype(F32)
        both_at = iota((TOK, C * MSG), 1)
        both_at = (both_at - MSG * lax.rem(lax.div(both_at, MSG), 2)).astype(F32)
        for l in range(TILES):
            out_row = [MSG * ids[:, j : j + 1] + rank[j] + CAP * l for j in range(TOP)]
            taken = (row_at == out_row[0]) | (row_at == out_row[1])
            pick_v[l * TOK : (l + 1) * TOK] = jnp.where(taken, 1.0, 0.0).astype(BF)
            back_row = [2 * MSG * ids[:, j : j + 1] + rank[j] + CAP * l for j in range(TOP)]
            comb_v[l] = (
                jnp.where(both_at == back_row[0], share[:, 0:1], 0.0)
                + jnp.where(both_at == back_row[1], share[:, 1:2], 0.0)
            ).astype(BF)

    @pl.when(active)
    def _():
        wait_bytes(prior_v.at[pl.ds(0, E - 1)], one_recv.at[ST2])

    @pl.when(jnp.logical_not(active))
    def _():
        wait_bytes(prior_v, one_recv.at[ST2])

    prior = prior_v[...].reshape(2 * HEAD, HEAD)
    for h in range(2):
        cols = slice(h * HEAD, (h + 1) * HEAD)
        entering = jnp.exp(-rates[h] * (place + 1.0))
        attended = inside[h] + mm(q_ref[:, cols], prior[h * HEAD : (h + 1) * HEAD]) * entering
        scale = lax.rsqrt(jnp.mean(attended * attended, axis=1, keepdims=True) + 1e-06)
        opening = jax.nn.sigmoid(og_ref[:, cols].astype(F32))
        ho_v[:, cols] = (attended * scale * opening).astype(BF)

    other_rows = pl.multiple_of(HALF * (1 - core), HALF)
    my_rows = pl.multiple_of(HALF * core, HALF)
    put(ho_v.at[pl.ds(other_rows, HALF)], hs_v, one_send.at[HO], one_recv.at[HO], c, sib)
    heads_here = ho_v[pl.ds(my_rows, HALF)]
    pltpu.make_async_copy(wout_hbm, wout_v.at[0], wl_sem.at[0]).wait()
    wait_bytes(wout_v.at[1], wr_sem.at[0])
    wait_bytes(hs_v, one_recv.at[HO])
    heads_there = hs_v[...]

    lead = 2 * z + side
    order = sorted(range(NZ), key=lambda i: -min(i, NZ - i))
    for i in order:
        zz = lax.rem(z + i, NZ)
        cols = pl.ds(pl.multiple_of(zz * SLAB, SLAB), SLAB)
        part = mm(heads_here, wout_v[0, :, cols]) + mm(heads_there, wout_v[1, :, cols])
        rst_v[i] = part.astype(BF)
        if i:
            put(rst_v.at[i], rsb_v.at[t], one_send.at[RS], one_recv.at[RS], c, 2 * zz + side)

    @pl.when(jnp.logical_not(active))
    def _():
        put(rst_v.at[0], rsb_v.at[t], one_send.at[RS], one_recv.at[RS], c, lead)

    @pl.when(active)
    def _():
        rsb_v[t] = rst_v[0]
        wait_bytes(rsb_v.at[pl.ds(0, NT - 1)], one_recv.at[RS])
        gain = gain_ref[pl.ds(pl.multiple_of(z * SLAB, SLAB), SLAB)].reshape(1, SLAB)
        for half in range(2):
            total = rsb_v[half].astype(F32)
            for zz in range(1, NZ):
                total = total + rsb_v[2 * zz + half].astype(F32)
            res_v[half * HALF : (half + 1) * HALF] = total
        scaled = (res_v[...] * gain).astype(BF)
        message = jnp.zeros((E * MSG, LANE), F32)
        for l in range(TILES):
            message = message + mm_t(
                pick_v[l * TOK : (l + 1) * TOK], scaled[:, l * LANE : (l + 1) * LANE]
            )
        mst_v[...] = message.astype(BF).reshape(E, MSG, LANE)

        def send_rows(i, carry):
            to = lax.rem(c + i, C)
            put(
                mst_v.at[lax.div(to, 2)],
                arr_v.at[mine],
                one_send.at[DISP],
                one_recv.at[DISP],
                to,
                t,
            )
            return carry

        lax.fori_loop(1, C, send_rows, 0)
        arr_v[mine] = mst_v[mine]
        wait_bytes(arr_v.at[pl.ds(0, E - 1)], one_recv.at[DISP])

    @pl.when(jnp.logical_not(active))
    def _():
        wait_bytes(arr_v, one_recv.at[DISP])

    arrived = arr_v[...].reshape(E * MSG, LANE)
    slot_row, at = iota((RQ, E * MSG), 0), iota((RQ, E * MSG), 1)
    slot_row = MSG * lax.div(slot_row, CAP) + lax.rem(slot_row, CAP)
    for l in range(TILES):
        spread = jnp.where(at == slot_row + CAP * l, 1.0, 0.0).astype(BF)
        x_v[z, :, l * LANE : (l + 1) * LANE] = mm(spread, arrived).astype(BF)

    def at_z(step):
        return lax.rem(z + step + 2 * NZ, NZ)

    def carried(step, way):
        return (way,) if step == H else (0, 1)

    def pass_on(step, way):
        turn = 1 if way == 0 else -1
        chunk = at_z(-turn * (step - 1))
        for p in carried(step, way):
            begin, size = parts[p]
            if step > 1:
                wait_bytes(
                    x_v.at[chunk, pl.ds(begin, size)], ag_recv.at[way, step - 2, p]
                )
            put(
                x_v.at[chunk, pl.ds(begin, size)],
                x_v.at[chunk, pl.ds(begin, size)],
                ag_send.at[way, step - 1, p],
                ag_recv.at[way, step - 1, p],
                c,
                2 * at_z(turn) + core,
            )

    def take(chunk, totals):
        x = x_v[chunk]
        rows = pl.ds(pl.multiple_of(chunk * SLAB, SLAB), SLAB)
        gain = gain_ref[rows].reshape(1, SLAB)
        wide = x.astype(F32) / gain
        squares = jnp.sum(wide * wide, axis=1, keepdims=True)
        new = [squares]
        for i in range(2):
            new.append(mm(x, wg_v[i, rows]))
            new.append(mm(x, wu_v[i, rows]))
        return [a + b for a, b in zip(totals, new)] if totals else new

    for way in range(2):
        pass_on(1, way)
    for n in (1, 2):
        src, dst = weights[n]
        pltpu.make_async_copy(src, dst.at[0], wl_sem.at[n]).wait()
        wait_bytes(dst.at[1], wr_sem.at[n])
    totals = take(z, None)
    for step in range(1, H + 1):
        for way in range(2):
            if step < H:
                pass_on(step + 1, way)
        for way in range(2):
            turn = 1 if way == 0 else -1
            chunk = at_z(-turn * step)
            gone = carried(step + 1, way) if step < H else ()
            for p in carried(step, way):
                if p not in gone:
                    begin, size = parts[p]
                    wait_bytes(
                        x_v.at[chunk, pl.ds(begin, size)], ag_recv.at[way, step - 1, p]
                    )
            if step < H:
                totals = take(chunk, totals)
        if step == H:
            totals = take(at_z(H), totals)

    inverse = lax.rsqrt(totals[0] / D + 1e-05)
    hidden = []
    for i in range(2):
        gate = totals[1 + 2 * i] * inverse
        up = totals[2 + 2 * i] * inverse
        hidden.append((jax.nn.silu(gate) * up).astype(BF))

    src, dst = weights[3]
    pltpu.make_async_copy(src, dst.at[0], wl_sem.at[3]).wait()
    wait_bytes(dst.at[1], wr_sem.at[3])

    def down(chunk):
        cols = pl.ds(pl.multiple_of(chunk * SLAB, SLAB), SLAB)
        return mm(hidden[0], wd_v[0, :, cols]) + mm(hidden[1], wd_v[1, :, cols])

    for step in range(1, H + 1):
        if step == 1:
            far = down(at_z(H))
            values = (far, far)
        else:
            values = (down(at_z(H + 1 - step)), down(at_z(-(H + 1 - step))))
        for way in range(2):
            turn = 1 if way == 0 else -1
            for p in (way,) if step == 1 else (way, 1 - way):
                begin, size = parts[p]
                value = values[way][begin : begin + size]
                if step > 2 or (step == 2 and p == way):
                    wait_bytes(
                        rp_v.at[way, step - 2, pl.ds(begin, size)],
                        rs_recv.at[way, step - 2, p],
                    )
                    value = value + rp_v[way, step - 2, pl.ds(begin, size)].astype(F32)
                sp_v[way, step - 1, pl.ds(begin, size)] = value.astype(BF)
                put(
                    sp_v.at[way, step - 1, pl.ds(begin, size)],
                    rp_v.at[way, step - 1, pl.ds(begin, size)],
                    rs_send.at[way, step - 1, p],
                    rs_recv.at[way, step - 1, p],
                    c,
                    2 * at_z(turn) + core,
                )
    own = down(z)
    pieces = []
    for p in range(2):
        begin, size = parts[p]
        value = own[begin : begin + size]
        for way in range(2):
            if H > 1 or p == way:
                wait_bytes(
                    rp_v.at[way, H - 1, pl.ds(begin, size)], rs_recv.at[way, H - 1, p]
                )
                value = value + rp_v[way, H - 1, pl.ds(begin, size)].astype(F32)
        pieces.append(value.astype(BF))
    final = jnp.concatenate(pieces, axis=0)

    slot_col, at = iota((E * MSG, RQ), 1), iota((E * MSG, RQ), 0)
    slot_col = MSG * lax.div(slot_col, CAP) + lax.rem(slot_col, CAP)
    message = jnp.zeros((E * MSG, LANE), F32)
    for l in range(TILES):
        gather = jnp.where(at == slot_col + CAP * l, 1.0, 0.0).astype(BF)
        message = message + mm(gather, final[:, l * LANE : (l + 1) * LANE])
    m2_v[...] = message.astype(BF).reshape(E, MSG, LANE)

    def send_back(i, carry):
        j = lax.rem(mine + i, E)
        put(m2_v.at[j], ret_v.at[c], one_send.at[RETN], one_recv.at[RETN], 2 * j + core, t)
        return carry

    lax.fori_loop(1, E, send_back, 0)

    @pl.when(jnp.logical_not(active))
    def _():
        send_back(0, 0)

    width = out_ref.shape[1]

    @pl.when(active)
    def _():
        ret_v[c] = m2_v[mine]
        wait_bytes(ret_v.at[pl.ds(0, C - 1)], one_recv.at[RETN])
        returned = ret_v[...].reshape(C * MSG, LANE)
        moe = jnp.concatenate([mm(comb_v[l], returned) for l in range(TILES)], axis=1)
        mixed = res_v[...] + moe
        low, high = mixed[:, :width].astype(BF), mixed[:, width:].astype(BF)
        fin_v[...] = jnp.where(core == 0, high, low)
        put(fin_v, out_ref, one_send.at[FIN], one_recv.at[FIN], c, sib)
        out_ref[...] = jnp.where(core == 0, low, high)

    @pl.when(active)
    def _():
        wait_bytes(state_v.at[pl.ds(0, E - 1)], one_send.at[ST1])
        wait_bytes(pst_v.at[pl.ds(0, C - 1)], one_send.at[ST2])
        wait_bytes(rst_v.at[pl.ds(0, NZ - 1)], one_send.at[RS])
        for _ in range(2):
            wait_bytes(mst_v.at[pl.ds(0, E - 1)], one_send.at[DISP])
        wait_bytes(mst_v.at[0], one_send.at[DISP])
        wait_bytes(m2_v.at[pl.ds(0, E - 1)], one_send.at[RETN])
        wait_bytes(fin_v, one_send.at[FIN])

    @pl.when(jnp.logical_not(active))
    def _():
        wait_bytes(state_v, one_send.at[ST1])
        wait_bytes(rst_v, one_send.at[RS])
        wait_bytes(m2_v, one_send.at[RETN])
        wait_bytes(out_ref, one_recv.at[FIN])

    wait_bytes(hs_v, one_send.at[HO])
    for n, (src, dst) in enumerate(weights):
        wait_bytes(dst.at[1], ws_sem.at[n])
    for way in range(2):
        for step in range(1, H + 1):
            for p in carried(step, way):
                begin, size = parts[p]
                wait_bytes(x_v.at[0, pl.ds(begin, size)], ag_send.at[way, step - 1, p])
            for p in (way,) if step == 1 else (0, 1):
                begin, size = parts[p]
                wait_bytes(
                    sp_v.at[way, step - 1, pl.ds(begin, size)], rs_send.at[way, step - 1, p]
                )


def local(C, NT, tokens, *args):
    (queries, key_rows, value_rows, out_gate, decay_index, w_out, norm_gain,
     expert_ids, gate_codes, w_gate, w_up, w_down) = args
    NZ = NT // 2
    H = NZ // 2
    E = C // 2
    PR = 2 * HEAD // E
    RQ = -(-E * CAP // 16) * 16
    D = NZ * SLAB
    vmem = pl.BlockSpec(memory_space=pltpu.VMEM)
    hbm = pl.BlockSpec(memory_space=pl.ANY)
    dma = pltpu.SemaphoreType.DMA
    return pl.pallas_call(
        functools.partial(kernel, C, NT, tokens),
        out_shape=jax.ShapeDtypeStruct((TOK, SLAB // 2), BF),
        in_specs=[pl.BlockSpec(memory_space=pltpu.SMEM)] + [vmem] * 7 + [hbm] * 4,
        out_specs=vmem,
        scratch_shapes=[
            pltpu.VMEM((2, 2 * HEAD, D), BF),
            pltpu.VMEM((2, D, UNITS), BF),
            pltpu.VMEM((2, D, UNITS), BF),
            pltpu.VMEM((2, UNITS, D), BF),
            pltpu.VMEM((E, PR, HEAD), BF),
            pltpu.VMEM((C, PR, HEAD), BF),
            pltpu.VMEM((C, PR, HEAD), BF),
            pltpu.VMEM((E, PR, HEAD), BF),
            pltpu.VMEM((TOK, 2 * HEAD), BF),
            pltpu.VMEM((HALF, 2 * HEAD), BF),
            pltpu.VMEM((NZ, HALF, SLAB), BF),
            pltpu.VMEM((NT, HALF, SLAB), BF),
            pltpu.VMEM((TILES * TOK, E * MSG), BF),
            pltpu.VMEM((TILES, TOK, C * MSG), BF),
            pltpu.VMEM((TOK, SLAB), F32),
            pltpu.VMEM((E, MSG, LANE), BF),
            pltpu.VMEM((E, MSG, LANE), BF),
            pltpu.VMEM((NZ, RQ, SLAB), BF),
            pltpu.VMEM((2, H, RQ, SLAB), BF),
            pltpu.VMEM((2, H, RQ, SLAB), BF),
            pltpu.VMEM((E, MSG, LANE), BF),
            pltpu.VMEM((C, MSG, LANE), BF),
            pltpu.VMEM((TOK, SLAB // 2), BF),
            dma((4,)),
            dma((4,)),
            dma((4,)),
            dma((7,)),
            dma((7,)),
            dma((2, H, 2)),
            dma((2, H, 2)),
            dma((2, H, 2)),
            dma((2, H, 2)),
        ],
        compiler_params=pltpu.CompilerParams(
            collective_id=0, has_side_effects=True, vmem_limit_bytes=48 * 2**20
        ),
        cost_estimate=pl.CostEstimate(
            flops=1_000_000_000, bytes_accessed=8_000_000, transcendentals=100_000
        ),
        name="layer",
    )(
        decay_index,
        queries,
        key_rows,
        value_rows,
        out_gate,
        norm_gain,
        expert_ids,
        gate_codes,
        w_out,
        w_gate,
        w_up,
        w_down,
    )


def solution(mesh):
    C, NT = mesh.shape["ctx"], mesh.shape["tp"]
    placed = (
        P("ctx", "tp"),
        P("ctx", "tp"),
        P("ctx", "tp"),
        P("ctx", "tp"),
        P("tp"),
        P("tp", None),
        P(),
        P("ctx", None),
        P("ctx", None),
        P("ctx", None, "tp"),
        P("ctx", None, "tp"),
        P("ctx", "tp", None),
    )

    def whole(*args):
        tokens = args[0].shape[0]
        return jax.shard_map(
            functools.partial(local, C, NT, tokens),
            mesh=mesh,
            in_specs=placed,
            out_specs=P("ctx", "tp"),
            check_vma=False,
        )(*args)

    return whole
```

```python
import functools

import jax
import jax.numpy as jnp
from jax import lax
from jax.experimental import pallas as pl
from jax.experimental.pallas import tpu as pltpu
from jax.sharding import PartitionSpec as P

HEAD = 128
TOP = 2
NLEV = 16
CAP = 9
TOK = 64
SLAB = 384
LANE = 128
TILES = SLAB // LANE
MSG = 32
UNITS = 144
WIDE = 256
PARTS = 3
NX = 4
MESH = pl.DeviceIdType.MESH
BF = jnp.bfloat16
F32 = jnp.float32


def mm(a, b):
    return jnp.dot(a, b, preferred_element_type=F32)


def mm_t(a, b):
    return lax.dot_general(a, b, (((0,), (0,)), ((), ())), preferred_element_type=F32)


def mm_nt(a, b):
    return lax.dot_general(a, b, (((1,), (1,)), ((), ())), preferred_element_type=F32)


def wait_bytes(ref, sem):
    pltpu.make_async_copy(ref, ref, sem).wait()


def iota(shape, dim):
    return lax.broadcasted_iota(jnp.int32, shape, dim)


def kernel(
    C,
    NT,
    TOKENS,
    idx_ref,
    q_hbm,
    k_hbm,
    v_hbm,
    og_hbm,
    gain_hbm,
    ids_hbm,
    codes_hbm,
    wout_hbm,
    wg_hbm,
    wu_hbm,
    wd_hbm,
    out_ref,
    q_ref,
    k_ref,
    v_ref,
    og_ref,
    gain_ref,
    ids_ref,
    codes_ref,
    wout_v,
    w1_v,
    wd_v,
    state_v,
    win_v,
    pst_v,
    prior_v,
    open_v,
    inside_v,
    ho_v,
    hs_v,
    rst_v,
    rsb_v,
    pick_v,
    comb_v,
    res_v,
    mst_v,
    arr_v,
    spread_v,
    gather_v,
    x_v,
    sum_v,
    square_v,
    sp_v,
    rp_v,
    m2_v,
    ret_v,
    fin_v,
    in_sem,
    wl_sem,
    ws_sem,
    wr_sem,
    one_send,
    one_recv,
    ag_send,
    ag_recv,
    rs_send,
    rs_recv,
):
    NZ = NT // 2
    H = NZ // 2
    E = C // 2
    PR = 2 * HEAD // E
    RQ = x_v.shape[1]
    D = NZ * SLAB
    NY = C // NX
    units = RQ // 16
    count = min(PARTS, units)
    edges = [16 * (units * p // count) for p in range(count + 1)]
    parts = [(a, b - a) for a, b in zip(edges, edges[1:])]
    split = (count + 1) // 2

    c = lax.axis_index("ctx")
    t = lax.axis_index("tp")
    z = lax.div(t, 2)
    core = lax.rem(t, 2)
    sib = t + 1 - 2 * core
    side = lax.rem(c, 2)
    mine = lax.div(c, 2)
    active = side == core
    idle = jnp.logical_not(active)
    y_at = lax.div(c, NX)
    x_at = lax.rem(c, NX)

    def away(k, n):
        half = lax.div(k + 1, 2)
        return lax.rem(n // 2 + jnp.where(lax.rem(k, 2) == 1, n - half, half), n)

    def everyone(i):
        to_y = lax.rem(y_at + away(lax.div(i, NX), NY), NY)
        return NX * to_y + lax.rem(x_at + away(lax.rem(i, NX), NX), NX)

    def pairs(i):
        hop = NX // 2 - 1 - lax.rem(i, NX // 2)
        to_y = lax.rem(y_at + away(lax.div(i, NX // 2), NY), NY)
        return NX // 2 * to_y + lax.rem(lax.div(x_at, 2) + hop, NX // 2)

    ST1, ST2, HO, RS, PAIR, DISP, RETN, FIN = range(8)

    def put(src, dst, send, recv, ctx, tp):
        pltpu.make_async_remote_copy(
            src_ref=src,
            dst_ref=dst,
            send_sem=send,
            recv_sem=recv,
            device_id={"ctx": ctx, "tp": tp},
            device_id_type=MESH,
        ).start()

    drains = []

    def later(ref, sem, when=None):
        drains.append((ref, sem, when))

    def finish():
        for ref, sem, when in drains:
            if when is None:
                wait_bytes(ref, sem)
            else:
                pl.when(when)(functools.partial(wait_bytes, ref, sem))

    inputs = (
        (k_hbm, k_ref),
        (v_hbm, v_ref),
        (q_hbm, q_ref),
        (og_hbm, og_ref),
        (ids_hbm, ids_ref),
        (codes_hbm, codes_ref),
        (gain_hbm, gain_ref),
    )
    loads = [
        pltpu.make_async_copy(src, dst, in_sem.at[n]) for n, (src, dst) in enumerate(inputs)
    ]
    for load in loads:
        load.start()

    barrier = pltpu.get_barrier_semaphore()

    def greet_ctx(i, carry):
        pl.semaphore_signal(
            barrier, inc=1, device_id={"ctx": everyone(i), "tp": t}, device_id_type=MESH
        )
        return carry

    def greet_tp(i, carry):
        pl.semaphore_signal(
            barrier, inc=1, device_id={"ctx": c, "tp": lax.rem(t + i, NT)}, device_id_type=MESH
        )
        return carry

    lax.fori_loop(0, C - 1, greet_ctx, 0)
    lax.fori_loop(1, NT, greet_tp, 0)

    def rows_of(ref, n):
        return ref.at[pl.ds(n * UNITS, UNITS)]

    weights = (
        (wout_hbm, wout_v.at[0], wout_v.at[1]),
        (wg_hbm.at[0], rows_of(w1_v, 0), rows_of(w1_v, 1)),
        (wu_hbm.at[0], rows_of(w1_v, 2), rows_of(w1_v, 3)),
        (wd_hbm.at[0], rows_of(wd_v, 0), rows_of(wd_v, 1)),
    )
    for n, (src, here, there) in enumerate(weights):
        pltpu.make_async_copy(src, here, wl_sem.at[n]).start()

    def have(n):
        src, here, there = weights[n]
        pltpu.make_async_copy(src, here, wl_sem.at[n]).wait()
        wait_bytes(there, wr_sem.at[n])

    log_fast = jnp.log(jnp.full((1, 1), 1.0 / 40.0, F32))
    log_slow = jnp.log(jnp.full((1, 1), 1.0 / (16.0 * TOKENS), F32))
    rates = []
    for h in range(2):
        fraction = jnp.full((1, 1), idx_ref[h].astype(F32), F32) / (NLEV - 1)
        rates.append(jnp.exp(log_fast + fraction * (log_slow - log_fast)))
    place = iota((TOK, 1), 0).astype(F32)
    loads[0].wait()
    loads[1].wait()
    for h in range(2):
        cols = slice(h * HEAD, (h + 1) * HEAD)
        fading = jnp.exp(-rates[h] * (TOK - 1.0 - place))
        faded = (k_ref[:, cols].astype(F32) * fading).astype(BF)
        state = mm_t(faded, v_ref[:, cols]).astype(BF)
        each = HEAD // PR
        state_v[h * each : (h + 1) * each] = state.reshape(each, PR, HEAD)

    pl.semaphore_wait(barrier, C - 1 + NT - 1)

    def send_piece(i, carry):
        j = pairs(i)
        put(
            state_v.at[j], win_v.at[c], one_send.at[ST1], one_recv.at[ST1], 2 * j + core, t
        )
        return carry

    lax.fori_loop(0, E - 1, send_piece, 0)

    @pl.when(idle)
    def _():
        send_piece(E - 1, 0)

    later(state_v.at[pl.ds(0, E - 1)], one_send.at[ST1], active)
    later(state_v, one_send.at[ST1], idle)
    for n, (src, here, there) in enumerate(weights):
        put(src, there, ws_sem.at[n], wr_sem.at[n], c, sib)
        later(there, ws_sem.at[n])

    for load in loads[2:]:
        load.wait()
    n_at, m_at = iota((TOK, TOK), 0), iota((TOK, TOK), 1)
    offsets = (n_at - m_at).astype(F32)
    for h in range(2):
        cols = slice(h * HEAD, (h + 1) * HEAD)
        scores = mm_nt(q_ref[:, cols], k_ref[:, cols])
        within = jnp.where(
            offsets >= 0.0, jnp.exp(-rates[h] * jnp.maximum(offsets, 0.0)), 0.0
        )
        inside_v[:, cols] = mm((scores * within).astype(BF), v_ref[:, cols])
    open_v[...] = jax.nn.sigmoid(og_ref[...].astype(F32))

    @pl.when(active)
    def _():
        win_v[c] = state_v[mine]
        wait_bytes(win_v.at[pl.ds(0, C - 1)], one_recv.at[ST1])
        first_head = mine * PR < HEAD
        decay = jnp.exp(-jnp.where(first_head, rates[0], rates[1]) * TOK)

        def turn(b, run):
            pst_v[b] = run.astype(BF)
            return run * decay + win_v[b].astype(F32)

        lax.fori_loop(0, C, turn, jnp.zeros((PR, HEAD), F32), unroll=True)

        def send_prefix(i, carry):
            to = everyone(i)
            put(pst_v.at[to], prior_v.at[mine], one_send.at[ST2], one_recv.at[ST2], to, t)
            return carry

        lax.fori_loop(0, C - 1, send_prefix, 0)
        prior_v[mine] = pst_v[c]

    later(pst_v.at[pl.ds(0, C - 1)], one_send.at[ST2], active)

    @pl.when(active)
    def _():
        eye = n_at == m_at

        def stand(row):
            return jnp.sum(jnp.where(eye, row, 0.0), axis=1, keepdims=True)

        def lie(column):
            return jnp.sum(jnp.where(eye, column, 0.0), axis=0, keepdims=True)

        ids = [stand(ids_ref[j : j + 1].astype(F32)) for j in range(TOP)]
        codes = [codes_ref[j : j + 1].astype(F32) for j in range(TOP)]
        share = [stand(codes[j] / (codes[0] + codes[1])) for j in range(TOP)]
        expert_at = iota((TOK, LANE), 1).astype(F32)
        hot = [jnp.where(expert_at == ids[j], 1.0, 0.0) for j in range(TOP)]
        before = jnp.where(n_at > m_at, 1.0, 0.0).astype(BF)
        ahead = mm(before, (hot[0] + hot[1]).astype(BF))
        rank = [jnp.sum(hot[j] * ahead, axis=1, keepdims=True) for j in range(TOP)]
        out_row = [lie(MSG * ids[j] + rank[j]) for j in range(TOP)]
        back_row = [2 * MSG * ids[j] + rank[j] for j in range(TOP)]
        row_at = iota((E * MSG, TOK), 0).astype(F32)
        both_at = iota((TOK, C * MSG), 1)
        both_at = (both_at - MSG * lax.rem(lax.div(both_at, MSG), 2)).astype(F32)
        for l in range(TILES):
            taken = (row_at == out_row[0] + CAP * l) | (row_at == out_row[1] + CAP * l)
            pick_v[:, l * TOK : (l + 1) * TOK] = jnp.where(taken, 1.0, 0.0).astype(BF)
            comb_v[l * TOK : (l + 1) * TOK] = (
                jnp.where(both_at == back_row[0] + CAP * l, share[0], 0.0)
                + jnp.where(both_at == back_row[1] + CAP * l, share[1], 0.0)
            ).astype(BF)

    slot_row, at = iota((RQ, E * MSG), 0), iota((RQ, E * MSG), 1)
    slot_row = MSG * lax.div(slot_row, CAP) + lax.rem(slot_row, CAP)
    for l in range(TILES):
        spread_v[l * RQ : (l + 1) * RQ] = jnp.where(at == slot_row + CAP * l, 1.0, 0.0).astype(BF)
    slot_col, at = iota((E * MSG, RQ), 1), iota((E * MSG, RQ), 0)
    slot_col = MSG * lax.div(slot_col, CAP) + lax.rem(slot_col, CAP)
    for l in range(TILES):
        gather_v[l] = jnp.where(at == slot_col + CAP * l, 1.0, 0.0).astype(BF)

    pl.when(active)(
        functools.partial(wait_bytes, prior_v.at[pl.ds(0, E - 1)], one_recv.at[ST2])
    )
    pl.when(idle)(functools.partial(wait_bytes, prior_v, one_recv.at[ST2]))
    prior = prior_v[...].reshape(2 * HEAD, HEAD)
    for h in range(2):
        cols = slice(h * HEAD, (h + 1) * HEAD)
        entering = jnp.exp(-rates[h] * (place + 1.0))
        attended = (
            inside_v[:, cols] + mm(q_ref[:, cols], prior[h * HEAD : (h + 1) * HEAD]) * entering
        )
        scale = lax.rsqrt(jnp.mean(attended * attended, axis=1, keepdims=True) + 1e-06)
        ho_v[:, cols] = (attended * scale * open_v[:, cols]).astype(BF)

    put(ho_v, hs_v, one_send.at[HO], one_recv.at[HO], c, sib)
    later(hs_v, one_send.at[HO])
    have(0)
    wait_bytes(hs_v, one_recv.at[HO])

    lead = 2 * z + side
    order = sorted(range(NZ), key=lambda i: -min(i, NZ - i))

    def project(begin, size):
        lanes = pl.ds(begin, size)
        for i in order:
            zz = lax.rem(z + i, NZ)
            cols = pl.ds(pl.multiple_of(zz * SLAB, SLAB) + begin, size)
            part = mm(ho_v[...], wout_v[0, :, cols]) + mm(hs_v[...], wout_v[1, :, cols])
            rst_v[i, :, :size] = part.astype(BF)
            if i:
                put(
                    rst_v.at[i, :, pl.ds(0, size)],
                    rsb_v.at[z, :, lanes],
                    one_send.at[RS],
                    one_recv.at[RS],
                    c,
                    2 * zz + side,
                )

        @pl.when(idle)
        def _():
            put(
                rst_v.at[0, :, pl.ds(0, size)],
                rsb_v.at[z, :, lanes],
                one_send.at[PAIR],
                one_recv.at[PAIR],
                c,
                lead,
            )

        @pl.when(active)
        def _():
            rsb_v[z, :, begin : begin + size] = rst_v[0, :, :size]

    for k, (begin, size) in enumerate(((0, WIDE), (WIDE, SLAB - WIDE))):
        here = core == k
        pl.when(here)(functools.partial(project, begin, size))
        later(rst_v.at[pl.ds(0, NZ - 1), :, pl.ds(0, size)], one_send.at[RS], here)
        later(rst_v.at[0, :, pl.ds(0, size)], one_send.at[PAIR], here & idle)

    @pl.when(active)
    def _():
        for k, size in enumerate((SLAB - WIDE, WIDE)):
            pl.when(core == k)(
                functools.partial(
                    wait_bytes, rsb_v.at[0, :, pl.ds(0, size)], one_recv.at[PAIR]
                )
            )
        wait_bytes(rsb_v.at[pl.ds(0, NZ - 1)], one_recv.at[RS])
        gain = gain_ref[pl.ds(pl.multiple_of(z * SLAB, SLAB), SLAB)].reshape(1, SLAB)
        total = rsb_v[0].astype(F32)
        for zz in range(1, NZ):
            total = total + rsb_v[zz].astype(F32)
        res_v[...] = total
        scaled = (total * gain).astype(BF)
        stacked = jnp.concatenate(
            [scaled[:, l * LANE : (l + 1) * LANE] for l in range(TILES)], axis=0
        )
        mst_v[...] = mm(pick_v[...], stacked).astype(BF).reshape(E, MSG, LANE)

        def send_rows(i, carry):
            to = everyone(i)
            put(
                mst_v.at[lax.div(to, 2)],
                arr_v.at[mine],
                one_send.at[DISP],
                one_recv.at[DISP],
                to,
                t,
            )
            return carry

        lax.fori_loop(0, C - 1, send_rows, 0)
        arr_v[mine] = mst_v[mine]
        wait_bytes(arr_v.at[pl.ds(0, E - 1)], one_recv.at[DISP])

    pl.when(idle)(functools.partial(wait_bytes, arr_v, one_recv.at[DISP]))
    for _ in range(2):
        later(mst_v.at[pl.ds(0, E - 1)], one_send.at[DISP], active)
    later(mst_v.at[0], one_send.at[DISP], active)

    spread = mm(spread_v[...], arr_v[...].reshape(E * MSG, LANE)).astype(BF)
    for l in range(TILES):
        x_v[z, :, l * LANE : (l + 1) * LANE] = spread[l * RQ : (l + 1) * RQ]

    def at_z(step):
        return lax.rem(z + step + 2 * NZ, NZ)

    def carried(step, way):
        if step < H:
            return range(count)
        return range(split) if way == 0 else range(split, count)

    def pass_on(step, way, p):
        turn = 1 - 2 * way
        begin, size = parts[p]
        piece = x_v.at[at_z(-turn * (step - 1)), pl.ds(begin, size)]
        put(
            piece,
            piece,
            ag_send.at[way, step - 1, p],
            ag_recv.at[way, step - 1, p],
            c,
            2 * at_z(turn) + core,
        )
        later(piece, ag_send.at[way, step - 1, p])

    def take(step):
        chunk = at_z(step)
        rows = pl.ds(pl.multiple_of(chunk * SLAB, SLAB), SLAB)
        x = x_v[chunk]
        new = mm_nt(x, w1_v[:, rows])
        wide = x.astype(F32) / gain_ref[rows].reshape(1, SLAB)
        wide = wide * wide
        squares = wide[:, :LANE]
        for l in range(1, TILES):
            squares = squares + wide[:, l * LANE : (l + 1) * LANE]
        if step == 0:
            sum_v[...] = new
            square_v[...] = squares
        else:
            sum_v[...] += new
            square_v[...] += squares

    for p in range(count):
        for way in range(2):
            if p in carried(1, way):
                pass_on(1, way, p)
    have(1)
    have(2)
    ready = [0]
    for step in range(1, H + 1):
        for p in range(count):
            for way in range(2):
                if p in carried(step, way):
                    begin, size = parts[p]
                    wait_bytes(
                        x_v.at[at_z((2 * way - 1) * step), pl.ds(begin, size)],
                        ag_recv.at[way, step - 1, p],
                    )
                    if step < H and p in carried(step + 1, way):
                        pass_on(step + 1, way, p)
            if ready:
                take(ready.pop(0))
        while ready:
            take(ready.pop(0))
        ready = [-step, step] if step < H else [H]
    take(H)

    inverse = lax.rsqrt(jnp.sum(square_v[...], axis=1, keepdims=True) / D + 1e-05)
    gate = sum_v[:, : 2 * UNITS] * inverse
    up = sum_v[:, 2 * UNITS :] * inverse
    hidden = (jax.nn.silu(gate) * up).astype(BF)
    have(3)

    def down(step):
        cols = pl.ds(pl.multiple_of(at_z(step) * SLAB, SLAB), SLAB)
        return mm(hidden, wd_v[:, cols])

    for step in range(1, H + 1):
        if step == 1:
            far = down(H)
            values = (far, far)
        else:
            values = (down(H + 1 - step), down(-(H + 1 - step)))
        for p in range(count):
            begin, size = parts[p]
            piece = pl.ds(begin, size)
            for way in range(2):
                if step == 1 and p not in carried(H, way):
                    continue
                value = values[way][begin : begin + size]
                if step > 2 or (step == 2 and p in carried(H, way)):
                    wait_bytes(rp_v.at[way, step - 2, piece], rs_recv.at[way, step - 2, p])
                    value = value + rp_v[way, step - 2, piece].astype(F32)
                sp_v[way, step - 1, piece] = value.astype(BF)
                put(
                    sp_v.at[way, step - 1, piece],
                    rp_v.at[way, step - 1, piece],
                    rs_send.at[way, step - 1, p],
                    rs_recv.at[way, step - 1, p],
                    c,
                    2 * at_z(1 - 2 * way) + core,
                )
                later(sp_v.at[way, step - 1, piece], rs_send.at[way, step - 1, p])
    own = down(0)
    pieces = []
    for p in range(count):
        begin, size = parts[p]
        piece = pl.ds(begin, size)
        value = own[begin : begin + size]
        for way in range(2):
            if H > 1 or p in carried(H, way):
                wait_bytes(rp_v.at[way, H - 1, piece], rs_recv.at[way, H - 1, p])
                value = value + rp_v[way, H - 1, piece].astype(F32)
        pieces.append(value.astype(BF))
    final = jnp.concatenate(pieces, axis=0)

    message = jnp.zeros((E * MSG, LANE), F32)
    for l in range(TILES):
        message = message + mm(gather_v[l], final[:, l * LANE : (l + 1) * LANE])
    m2_v[...] = message.astype(BF).reshape(E, MSG, LANE)

    def send_back(i, carry):
        j = pairs(i)
        put(m2_v.at[j], ret_v.at[c], one_send.at[RETN], one_recv.at[RETN], 2 * j + core, t)
        return carry

    lax.fori_loop(0, E - 1, send_back, 0)

    @pl.when(idle)
    def _():
        send_back(E - 1, 0)

    later(m2_v.at[pl.ds(0, E - 1)], one_send.at[RETN], active)
    later(m2_v, one_send.at[RETN], idle)
    width = out_ref.shape[1]

    @pl.when(active)
    def _():
        ret_v[c] = m2_v[mine]
        wait_bytes(ret_v.at[pl.ds(0, C - 1)], one_recv.at[RETN])
        tall = mm(comb_v[...], ret_v[...].reshape(C * MSG, LANE))
        moe = jnp.concatenate([tall[l * TOK : (l + 1) * TOK] for l in range(TILES)], axis=1)
        mixed = res_v[...] + moe
        low, high = mixed[:, :width].astype(BF), mixed[:, width:].astype(BF)
        fin_v[...] = jnp.where(core == 0, high, low)
        put(fin_v, out_ref, one_send.at[FIN], one_recv.at[FIN], c, sib)
        out_ref[...] = jnp.where(core == 0, low, high)

    later(fin_v, one_send.at[FIN], active)
    later(out_ref, one_recv.at[FIN], idle)
    finish()


def local(C, NT, tokens, *args):
    (queries, key_rows, value_rows, out_gate, decay_index, w_out, norm_gain,
     expert_ids, gate_codes, w_gate, w_up, w_down) = args
    NZ = NT // 2
    H = NZ // 2
    E = C // 2
    PR = 2 * HEAD // E
    RQ = -(-E * CAP // 16) * 16
    D = NZ * SLAB
    vmem = pl.BlockSpec(memory_space=pltpu.VMEM)
    hbm = pl.BlockSpec(memory_space=pltpu.HBM)
    dma = pltpu.SemaphoreType.DMA
    return pl.pallas_call(
        functools.partial(kernel, C, NT, tokens),
        out_shape=jax.ShapeDtypeStruct((TOK, SLAB // 2), BF),
        in_specs=[pl.BlockSpec(memory_space=pltpu.SMEM)] + [hbm] * 11,
        out_specs=vmem,
        scratch_shapes=[
            pltpu.VMEM((TOK, 2 * HEAD), BF),
            pltpu.VMEM((TOK, 2 * HEAD), BF),
            pltpu.VMEM((TOK, 2 * HEAD), BF),
            pltpu.VMEM((TOK, 2 * HEAD), BF),
            pltpu.VMEM((D,), F32),
            pltpu.VMEM((TOP, TOK), jnp.int32),
            pltpu.VMEM((TOP, TOK), jnp.int32),
            pltpu.VMEM((2, 2 * HEAD, D), BF),
            pltpu.VMEM((4 * UNITS, D), BF),
            pltpu.VMEM((2 * UNITS, D), BF),
            pltpu.VMEM((E, PR, HEAD), BF),
            pltpu.VMEM((C, PR, HEAD), BF),
            pltpu.VMEM((C, PR, HEAD), BF),
            pltpu.VMEM((E, PR, HEAD), BF),
            pltpu.VMEM((TOK, 2 * HEAD), F32),
            pltpu.VMEM((TOK, 2 * HEAD), F32),
            pltpu.VMEM((TOK, 2 * HEAD), BF),
            pltpu.VMEM((TOK, 2 * HEAD), BF),
            pltpu.VMEM((NZ, TOK, WIDE), BF),
            pltpu.VMEM((NZ, TOK, SLAB), BF),
            pltpu.VMEM((E * MSG, TILES * TOK), BF),
            pltpu.VMEM((TILES * TOK, C * MSG), BF),
            pltpu.VMEM((TOK, SLAB), F32),
            pltpu.VMEM((E, MSG, LANE), BF),
            pltpu.VMEM((E, MSG, LANE), BF),
            pltpu.VMEM((TILES * RQ, E * MSG), BF),
            pltpu.VMEM((TILES, E * MSG, RQ), BF),
            pltpu.VMEM((NZ, RQ, SLAB), BF),
            pltpu.VMEM((RQ, 4 * UNITS), F32),
            pltpu.VMEM((RQ, LANE), F32),
            pltpu.VMEM((2, H, RQ, SLAB), BF),
            pltpu.VMEM((2, H, RQ, SLAB), BF),
            pltpu.VMEM((E, MSG, LANE), BF),
            pltpu.VMEM((C, MSG, LANE), BF),
            pltpu.VMEM((TOK, SLAB // 2), BF),
            dma((7,)),
            dma((4,)),
            dma((4,)),
            dma((4,)),
            dma((8,)),
            dma((8,)),
            dma((2, H, PARTS)),
            dma((2, H, PARTS)),
            dma((2, H, PARTS)),
            dma((2, H, PARTS)),
        ],
        compiler_params=pltpu.CompilerParams(
            collective_id=0, has_side_effects=True, vmem_limit_bytes=60 * 2**20
        ),
        cost_estimate=pl.CostEstimate(
            flops=1_000_000_000, bytes_accessed=8_000_000, transcendentals=100_000
        ),
        name="layer",
    )(
        decay_index,
        queries,
        key_rows,
        value_rows,
        out_gate,
        norm_gain,
        expert_ids.T,
        gate_codes.T,
        w_out,
        w_gate.transpose(0, 2, 1),
        w_up.transpose(0, 2, 1),
        w_down,
    )


def solution(mesh):
    C, NT = mesh.shape["ctx"], mesh.shape["tp"]
    placed = (
        P("ctx", "tp"),
        P("ctx", "tp"),
        P("ctx", "tp"),
        P("ctx", "tp"),
        P("tp"),
        P("tp", None),
        P(),
        P("ctx", None),
        P("ctx", None),
        P("ctx", None, "tp"),
        P("ctx", None, "tp"),
        P("ctx", "tp", None),
    )

    def whole(*args):
        tokens = args[0].shape[0]
        return jax.shard_map(
            functools.partial(local, C, NT, tokens),
            mesh=mesh,
            in_specs=placed,
            out_specs=P("ctx", "tp"),
            check_vma=False,
        )(*args)

    return whole
```

```python
import functools

import jax
import jax.numpy as jnp
from jax import lax
from jax.experimental import pallas as pl
from jax.experimental.pallas import tpu as pltpu
from jax.sharding import PartitionSpec as P

HEAD = 128
TOP = 2
NLEV = 16
CAP = 9
TOK = 64
SLAB = 384
LANE = 128
TILES = SLAB // LANE
MSG = 32
UNITS = 144
WIDE = 256
PARTS = 4
NX = 4
MESH = pl.DeviceIdType.MESH
BF = jnp.bfloat16
F32 = jnp.float32


def mm(a, b):
    return jnp.dot(a, b, preferred_element_type=F32)


def mm_t(a, b):
    return lax.dot_general(a, b, (((0,), (0,)), ((), ())), preferred_element_type=F32)


def mm_nt(a, b):
    return lax.dot_general(a, b, (((1,), (1,)), ((), ())), preferred_element_type=F32)


def wait_bytes(ref, sem):
    pltpu.make_async_copy(ref, ref, sem).wait()


def iota(shape, dim):
    return lax.broadcasted_iota(jnp.int32, shape, dim)


def kernel(
    C,
    NT,
    TOKENS,
    idx_ref,
    q_hbm,
    k_hbm,
    v_hbm,
    og_hbm,
    gain_hbm,
    ids_hbm,
    codes_hbm,
    wout_hbm,
    wg_hbm,
    wu_hbm,
    wd_hbm,
    out_ref,
    q_ref,
    k_ref,
    v_ref,
    og_ref,
    gain_ref,
    ids_ref,
    codes_ref,
    wout_v,
    w1_v,
    wd_v,
    state_v,
    win_v,
    pst_v,
    prior_v,
    open_v,
    inside_v,
    enter_v,
    ho_v,
    hs_v,
    rst_v,
    rsb_v,
    pick_v,
    comb_v,
    res_v,
    mst_v,
    arr_v,
    spread_v,
    gather_v,
    x_v,
    sum_v,
    square_v,
    hidden_v,
    last_v,
    sp_v,
    rp_v,
    m2_v,
    ret_v,
    fin_v,
    in_sem,
    wl_sem,
    ws_sem,
    wr_sem,
    one_send,
    one_recv,
    disp_recv,
    ag_send,
    ag_recv,
    rs_send,
    rs_recv,
):
    NZ = NT // 2
    H = NZ // 2
    E = C // 2
    PR = 2 * HEAD // E
    RQ = x_v.shape[1]
    D = NZ * SLAB
    NY = C // NX
    units = RQ // 16
    count = min(PARTS, units)
    edges = [16 * (units * p // count) for p in range(count + 1)]
    parts = [(a, b - a) for a, b in zip(edges, edges[1:])]
    split = (count + 1) // 2
    begins = [e // CAP for e in edges[:-1]]
    reach = [0] + [min(E, -(-e // CAP)) for e in edges[1:]]
    whole = [0] + [min(E, e // CAP) for e in edges[1:]]

    c = lax.axis_index("ctx")
    t = lax.axis_index("tp")
    z = lax.div(t, 2)
    core = lax.rem(t, 2)
    sib = t + 1 - 2 * core
    side = lax.rem(c, 2)
    mine = lax.div(c, 2)
    active = side == core
    idle = jnp.logical_not(active)
    y_at = lax.div(c, NX)
    x_at = lax.rem(c, NX)

    def away(k, n):
        half = lax.div(k + 1, 2)
        return lax.rem(n // 2 + jnp.where(lax.rem(k, 2) == 1, n - half, half), n)

    def everyone(i):
        to_y = lax.rem(y_at + away(lax.div(i, NX), NY), NY)
        return NX * to_y + lax.rem(x_at + away(lax.rem(i, NX), NX), NX)

    def pairs(i):
        hop = NX // 2 - 1 - lax.rem(i, NX // 2)
        to_y = lax.rem(y_at + away(lax.div(i, NX // 2), NY), NY)
        return NX // 2 * to_y + lax.rem(lax.div(x_at, 2) + hop, NX // 2)

    def slot_at(to):
        far = lax.rem(y_at - lax.div(to, NX) + NY, NY)
        rank = jnp.where(
            far == 0, 0, jnp.where(far <= NY // 2, 2 * far - 1, 2 * (NY - far))
        )
        return NX // 2 * rank + lax.div(x_at, 2)

    def block_of(slot):
        rank = lax.div(slot, NX // 2)
        half = lax.div(rank + 1, 2)
        far = jnp.where(lax.rem(rank, 2) == 1, half, NY - half)
        return NX * lax.rem(y_at + far, NY) + core + 2 * lax.rem(slot, NX // 2)

    own_slot = lax.div(x_at, 2)

    ST1, ST2, HO, RS, PAIR, DISP, RETN, FIN = range(8)

    def put(src, dst, send, recv, ctx, tp):
        pltpu.make_async_remote_copy(
            src_ref=src,
            dst_ref=dst,
            send_sem=send,
            recv_sem=recv,
            device_id={"ctx": ctx, "tp": tp},
            device_id_type=MESH,
        ).start()

    drains = []

    def later(ref, sem, when=None):
        drains.append((ref, sem, when))

    def finish():
        for ref, sem, when in drains:
            if when is None:
                wait_bytes(ref, sem)
            else:
                pl.when(when)(functools.partial(wait_bytes, ref, sem))
        drains.clear()

    inputs = (
        (k_hbm, k_ref),
        (v_hbm, v_ref),
        (q_hbm, q_ref),
        (og_hbm, og_ref),
        (ids_hbm, ids_ref),
        (codes_hbm, codes_ref),
        (gain_hbm, gain_ref),
    )
    loads = [
        pltpu.make_async_copy(src, dst, in_sem.at[n]) for n, (src, dst) in enumerate(inputs)
    ]
    for load in loads:
        load.start()

    barrier = pltpu.get_barrier_semaphore()

    def greet_ctx(i, carry):
        pl.semaphore_signal(
            barrier, inc=1, device_id={"ctx": everyone(i), "tp": t}, device_id_type=MESH
        )
        return carry

    def greet_tp(i, carry):
        pl.semaphore_signal(
            barrier, inc=1, device_id={"ctx": c, "tp": lax.rem(t + i, NT)}, device_id_type=MESH
        )
        return carry

    lax.fori_loop(0, C - 1, greet_ctx, 0)
    lax.fori_loop(1, NT, greet_tp, 0)

    def rows_of(ref, n):
        return ref.at[pl.ds(n * UNITS, UNITS)]

    weights = (
        (wout_hbm, wout_v.at[0], wout_v.at[1]),
        (wg_hbm.at[0], rows_of(w1_v, 0), rows_of(w1_v, 1)),
        (wu_hbm.at[0], rows_of(w1_v, 2), rows_of(w1_v, 3)),
        (wd_hbm.at[0], rows_of(wd_v, 0), rows_of(wd_v, 1)),
    )
    for n, (src, here, there) in enumerate(weights):
        pltpu.make_async_copy(src, here, wl_sem.at[n]).start()

    def have(n):
        src, here, there = weights[n]
        pltpu.make_async_copy(src, here, wl_sem.at[n]).wait()
        wait_bytes(there, wr_sem.at[n])

    log_fast = jnp.log(jnp.full((1, 1), 1.0 / 40.0, F32))
    log_slow = jnp.log(jnp.full((1, 1), 1.0 / (16.0 * TOKENS), F32))
    rates = []
    for h in range(2):
        fraction = jnp.full((1, 1), idx_ref[h].astype(F32), F32) / (NLEV - 1)
        rates.append(jnp.exp(log_fast + fraction * (log_slow - log_fast)))
    place = iota((TOK, 1), 0).astype(F32)
    loads[0].wait()
    loads[1].wait()
    for h in range(2):
        cols = slice(h * HEAD, (h + 1) * HEAD)
        fading = jnp.exp(-rates[h] * (TOK - 1.0 - place))
        faded = (k_ref[:, cols].astype(F32) * fading).astype(BF)
        state = mm_t(faded, v_ref[:, cols]).astype(BF)
        each = HEAD // PR
        state_v[h * each : (h + 1) * each] = state.reshape(each, PR, HEAD)

    pl.semaphore_wait(barrier, C - 1 + NT - 1)

    def send_piece(i, carry):
        j = pairs(i)
        put(
            state_v.at[j], win_v.at[c], one_send.at[ST1], one_recv.at[ST1], 2 * j + core, t
        )
        return carry

    lax.fori_loop(0, E - 1, send_piece, 0)

    @pl.when(idle)
    def _():
        send_piece(E - 1, 0)

    later(state_v.at[pl.ds(0, E - 1)], one_send.at[ST1], active)
    later(state_v, one_send.at[ST1], idle)
    for n, (src, here, there) in enumerate(weights):
        put(src, there, ws_sem.at[n], wr_sem.at[n], c, sib)
        later(there, ws_sem.at[n])

    for load in loads[2:]:
        load.wait()
    n_at, m_at = iota((TOK, TOK), 0), iota((TOK, TOK), 1)
    offsets = (n_at - m_at).astype(F32)
    for h in range(2):
        cols = slice(h * HEAD, (h + 1) * HEAD)
        scores = mm_nt(q_ref[:, cols], k_ref[:, cols])
        within = jnp.where(
            offsets >= 0.0, jnp.exp(-rates[h] * jnp.maximum(offsets, 0.0)), 0.0
        )
        inside_v[:, cols] = mm((scores * within).astype(BF), v_ref[:, cols])
    open_v[...] = jax.nn.sigmoid(og_ref[...].astype(F32))
    enter_v[...] = jnp.concatenate(
        [
            jnp.broadcast_to(jnp.exp(-rates[h] * (place + 1.0)), (TOK, HEAD))
            for h in range(2)
        ],
        axis=1,
    )

    @pl.when(active)
    def _():
        win_v[c] = state_v[mine]
        wait_bytes(win_v.at[pl.ds(0, C - 1)], one_recv.at[ST1])
        first_head = mine * PR < HEAD
        decay = jnp.exp(-jnp.where(first_head, rates[0], rates[1]) * TOK)

        def turn(b, run):
            pst_v[b] = run.astype(BF)
            return run * decay + win_v[b].astype(F32)

        lax.fori_loop(0, C, turn, jnp.zeros((PR, HEAD), F32), unroll=True)

        def send_prefix(i, carry):
            to = everyone(i)
            put(pst_v.at[to], prior_v.at[mine], one_send.at[ST2], one_recv.at[ST2], to, t)
            return carry

        lax.fori_loop(0, C - 1, send_prefix, 0)
        prior_v[mine] = pst_v[c]

    later(pst_v.at[pl.ds(0, C - 1)], one_send.at[ST2], active)

    @pl.when(active)
    def _():
        eye = n_at == m_at

        def stand(row):
            return jnp.sum(jnp.where(eye, row, 0.0), axis=1, keepdims=True)

        def lie(column):
            return jnp.sum(jnp.where(eye, column, 0.0), axis=0, keepdims=True)

        ids = [stand(ids_ref[j : j + 1].astype(F32)) for j in range(TOP)]
        codes = [codes_ref[j : j + 1].astype(F32) for j in range(TOP)]
        share = [stand(codes[j] / (codes[0] + codes[1])) for j in range(TOP)]
        expert_at = iota((TOK, LANE), 1).astype(F32)
        hot = [jnp.where(expert_at == ids[j], 1.0, 0.0) for j in range(TOP)]
        before = jnp.where(n_at > m_at, 1.0, 0.0).astype(BF)
        ahead = mm(before, (hot[0] + hot[1]).astype(BF))
        rank = [jnp.sum(hot[j] * ahead, axis=1, keepdims=True) for j in range(TOP)]
        out_row = [lie(MSG * ids[j] + rank[j]) for j in range(TOP)]
        back_row = [2 * MSG * ids[j] + rank[j] for j in range(TOP)]
        row_at = iota((E * MSG, TOK), 0).astype(F32)
        both_at = iota((TOK, C * MSG), 1)
        both_at = (both_at - MSG * lax.rem(lax.div(both_at, MSG), 2)).astype(F32)
        for l in range(TILES):
            taken = (row_at == out_row[0] + CAP * l) | (row_at == out_row[1] + CAP * l)
            pick_v[:, l * TOK : (l + 1) * TOK] = jnp.where(taken, 1.0, 0.0).astype(BF)
            comb_v[l * TOK : (l + 1) * TOK] = (
                jnp.where(both_at == back_row[0] + CAP * l, share[0], 0.0)
                + jnp.where(both_at == back_row[1] + CAP * l, share[1], 0.0)
            ).astype(BF)

    for p, (begin, size) in enumerate(parts):
        deep = MSG * (reach[p + 1] - begins[p])
        if deep:
            row, at = begin + iota((size, deep), 0), iota((size, deep), 1)
            row = MSG * (lax.div(row, CAP) - begins[p]) + lax.rem(row, CAP)
            for l in range(TILES):
                start = TILES * begin + l * size
                spread_v[start : start + size, :deep] = jnp.where(
                    at == row + CAP * l, 1.0, 0.0
                ).astype(BF)
        low, high = whole[p], whole[p + 1]
        if low < high:
            base = CAP * low // 16 * 16
            shape = (MSG * (high - low), edges[p + 1] - base)
            at, row = MSG * low + iota(shape, 0), base + iota(shape, 1)
            row = MSG * lax.div(row, CAP) + lax.rem(row, CAP)
            for l in range(TILES):
                gather_v[l, MSG * low : MSG * high, : shape[1]] = jnp.where(
                    at == row + CAP * l, 1.0, 0.0
                ).astype(BF)

    pl.when(active)(
        functools.partial(wait_bytes, prior_v.at[pl.ds(0, E - 1)], one_recv.at[ST2])
    )
    pl.when(idle)(functools.partial(wait_bytes, prior_v, one_recv.at[ST2]))
    prior = prior_v[...].reshape(2 * HEAD, HEAD)
    for h in range(2):
        cols = slice(h * HEAD, (h + 1) * HEAD)
        outside = mm(q_ref[:, cols], prior[h * HEAD : (h + 1) * HEAD])
        attended = inside_v[:, cols] + outside * enter_v[:, cols]
        scale = lax.rsqrt(jnp.mean(attended * attended, axis=1, keepdims=True) + 1e-06)
        ho_v[:, cols] = (attended * scale * open_v[:, cols]).astype(BF)

    put(ho_v, hs_v, one_send.at[HO], one_recv.at[HO], c, sib)
    later(hs_v, one_send.at[HO])
    have(0)
    wait_bytes(hs_v, one_recv.at[HO])

    lead = 2 * z + side
    order = sorted(range(NZ), key=lambda i: -min(i, NZ - i))

    def project(begin, size):
        lanes = pl.ds(begin, size)
        for i in order:
            zz = lax.rem(z + i, NZ)
            cols = pl.ds(pl.multiple_of(zz * SLAB, SLAB) + begin, size)
            part = mm(ho_v[...], wout_v[0, :, cols]) + mm(hs_v[...], wout_v[1, :, cols])
            rst_v[i, :, :size] = part.astype(BF)
            if i:
                put(
                    rst_v.at[i, :, pl.ds(0, size)],
                    rsb_v.at[z, :, lanes],
                    one_send.at[RS],
                    one_recv.at[RS],
                    c,
                    2 * zz + side,
                )

        @pl.when(idle)
        def _():
            put(
                rst_v.at[0, :, pl.ds(0, size)],
                rsb_v.at[z, :, lanes],
                one_send.at[PAIR],
                one_recv.at[PAIR],
                c,
                lead,
            )

        @pl.when(active)
        def _():
            rsb_v[z, :, begin : begin + size] = rst_v[0, :, :size]

    for k, (begin, size) in enumerate(((0, WIDE), (WIDE, SLAB - WIDE))):
        here = core == k
        pl.when(here)(functools.partial(project, begin, size))
        later(rst_v.at[pl.ds(0, NZ - 1), :, pl.ds(0, size)], one_send.at[RS], here)
        later(rst_v.at[0, :, pl.ds(0, size)], one_send.at[PAIR], here & idle)

    @pl.when(active)
    def _():
        for k, size in enumerate((SLAB - WIDE, WIDE)):
            pl.when(core == k)(
                functools.partial(
                    wait_bytes, rsb_v.at[0, :, pl.ds(0, size)], one_recv.at[PAIR]
                )
            )
        wait_bytes(rsb_v.at[pl.ds(0, NZ - 1)], one_recv.at[RS])
        gain = gain_ref[pl.ds(pl.multiple_of(z * SLAB, SLAB), SLAB)].reshape(1, SLAB)
        total = rsb_v[0].astype(F32)
        for zz in range(1, NZ):
            total = total + rsb_v[zz].astype(F32)
        res_v[...] = total
        scaled = (total * gain).astype(BF)
        stacked = jnp.concatenate(
            [scaled[:, l * LANE : (l + 1) * LANE] for l in range(TILES)], axis=0
        )
        mst_v[...] = mm(pick_v[...], stacked).astype(BF).reshape(E, MSG, LANE)

        def send_rows(i, carry):
            to = everyone(i)
            slot = slot_at(to)
            group = sum((slot >= r).astype(jnp.int32) for r in reach[1:-1])
            put(
                mst_v.at[lax.div(to, 2)],
                arr_v.at[slot],
                one_send.at[DISP],
                disp_recv.at[group],
                to,
                t,
            )
            return carry

        lax.fori_loop(0, C - 1, send_rows, 0)
        arr_v[own_slot] = mst_v[mine]

    for _ in range(2):
        later(mst_v.at[pl.ds(0, E - 1)], one_send.at[DISP], active)
    later(mst_v.at[0], one_send.at[DISP], active)

    def at_z(step):
        return lax.rem(z + step + 2 * NZ, NZ)

    def carried(step, way):
        if step < H:
            return range(count)
        return range(split) if way == 0 else range(split, count)

    def pass_on(step, way, p):
        turn = 1 - 2 * way
        begin, size = parts[p]
        piece = x_v.at[at_z(-turn * (step - 1)), pl.ds(begin, size)]
        put(
            piece,
            piece,
            ag_send.at[way, step - 1, p],
            ag_recv.at[way, step - 1, p],
            c,
            2 * at_z(turn) + core,
        )
        later(piece, ag_send.at[way, step - 1, p])

    def take(step, p=None):
        chunk = at_z(step)
        cols = pl.ds(pl.multiple_of(chunk * SLAB, SLAB), SLAB)
        begin, size = (0, RQ) if p is None else parts[p]
        rows = pl.ds(begin, size)
        x = x_v[chunk, rows]
        new = mm_nt(x, w1_v[:, cols])
        wide = x.astype(F32) * (1.0 / gain_ref[cols].reshape(1, SLAB))
        wide = wide * wide
        squares = wide[:, :LANE]
        for l in range(1, TILES):
            squares = squares + wide[:, l * LANE : (l + 1) * LANE]
        if step == 0:
            sum_v[rows] = new
            square_v[rows] = squares
        elif p is None:
            sum_v[rows] += new
            square_v[rows] += squares
        else:
            return sum_v[rows] + new, square_v[rows] + squares

    def down(step, hidden):
        cols = pl.ds(pl.multiple_of(at_z(step) * SLAB, SLAB), SLAB)
        return mm(hidden, wd_v[:, cols])

    def add_up(step, way, p, value):
        begin, size = parts[p]
        piece = pl.ds(begin, size)
        sp_v[way, step - 1, piece] = value.astype(BF)
        put(
            sp_v.at[way, step - 1, piece],
            rp_v.at[way, step - 1, piece],
            rs_send.at[way, step - 1, p],
            rs_recv.at[way, step - 1, p],
            c,
            2 * at_z(1 - 2 * way) + core,
        )
        later(sp_v.at[way, step - 1, piece], rs_send.at[way, step - 1, p])

    for p, (begin, size) in enumerate(parts):
        low, high = reach[p], reach[p + 1]
        if low < high:
            if p == 0:
                pl.when(active)(
                    functools.partial(
                        wait_bytes, arr_v.at[pl.ds(0, high - 1)], disp_recv.at[0]
                    )
                )
                pl.when(idle)(
                    functools.partial(wait_bytes, arr_v.at[pl.ds(0, high)], disp_recv.at[0])
                )
            else:
                wait_bytes(arr_v.at[pl.ds(low, high - low)], disp_recv.at[p])
        deep = MSG * (high - begins[p])
        if deep:
            rows = arr_v[begins[p] : high].reshape(deep, LANE)
            start = TILES * begin
            spread = mm(spread_v[start : start + TILES * size, :deep], rows).astype(BF)
            for l in range(TILES):
                x_v[z, begin : begin + size, l * LANE : (l + 1) * LANE] = spread[
                    l * size : (l + 1) * size
                ]
        else:
            x_v[z, begin : begin + size] = jnp.zeros((size, SLAB), BF)
        for way in range(2):
            if p in carried(1, way):
                pass_on(1, way, p)
    have(1)
    have(2)
    ready = [0]
    for step in range(1, H):
        for p in range(count):
            for way in range(2):
                begin, size = parts[p]
                wait_bytes(
                    x_v.at[at_z((2 * way - 1) * step), pl.ds(begin, size)],
                    ag_recv.at[way, step - 1, p],
                )
                if p in carried(step + 1, way):
                    pass_on(step + 1, way, p)
            if ready:
                take(ready.pop(0))
        while ready:
            take(ready.pop(0))
        ready = [-step, step]
    while ready:
        take(ready.pop(0))
    have(3)

    for p in sorted(range(count), key=lambda p: p if p < split else p - split + 0.5):
        way = 0 if p < split else 1
        begin, size = parts[p]
        wait_bytes(x_v.at[at_z(H), pl.ds(begin, size)], ag_recv.at[way, H - 1, p])
        sums, squares = take(H, p)
        inverse = lax.rsqrt(jnp.sum(squares, axis=1, keepdims=True) / D + 1e-05)
        gate = sums[:, : 2 * UNITS] * inverse
        up = sums[:, 2 * UNITS :] * inverse
        hidden = (jax.nn.silu(gate) * up).astype(BF)
        hidden_v[begin : begin + size] = hidden
        add_up(1, way, p, down(H, hidden))

    for step in range(2, H + 1):
        values = (down(H + 1 - step, hidden_v[...]), down(step - H - 1, hidden_v[...]))
        for p in range(count):
            begin, size = parts[p]
            piece = pl.ds(begin, size)
            for way in range(2):
                value = values[way][begin : begin + size]
                if step > 2 or p in carried(H, way):
                    wait_bytes(rp_v.at[way, step - 2, piece], rs_recv.at[way, step - 2, p])
                    value = value + rp_v[way, step - 2, piece].astype(F32)
                add_up(step, way, p, value)

    own = down(0, hidden_v[...])

    def send_back(slot, carry):
        @pl.when(jnp.logical_not(active & (slot == own_slot)))
        def _():
            put(
                m2_v.at[slot],
                ret_v.at[c],
                one_send.at[RETN],
                one_recv.at[RETN],
                block_of(slot),
                t,
            )

        return carry

    for p, (begin, size) in enumerate(parts):
        piece = pl.ds(begin, size)
        value = own[begin : begin + size]
        for way in range(2):
            if H > 1 or p in carried(H, way):
                wait_bytes(rp_v.at[way, H - 1, piece], rs_recv.at[way, H - 1, p])
                value = value + rp_v[way, H - 1, piece].astype(F32)
        last_v[piece] = value.astype(BF)
        low, high = whole[p], whole[p + 1]
        if low < high:
            base = CAP * low // 16 * 16
            deep = edges[p + 1] - base
            message = jnp.zeros((MSG * (high - low), LANE), F32)
            for l in range(TILES):
                message = message + mm(
                    gather_v[l, MSG * low : MSG * high, :deep],
                    last_v[base : base + deep, l * LANE : (l + 1) * LANE],
                )
            m2_v[low:high] = message.astype(BF).reshape(high - low, MSG, LANE)
            lax.fori_loop(low, high, send_back, 0)
    finish()
    later(m2_v.at[pl.ds(0, E - 1)], one_send.at[RETN], active)
    later(m2_v, one_send.at[RETN], idle)
    width = out_ref.shape[1]

    @pl.when(active)
    def _():
        ret_v[c] = m2_v[own_slot]
        wait_bytes(ret_v.at[pl.ds(0, C - 1)], one_recv.at[RETN])
        tall = mm(comb_v[...], ret_v[...].reshape(C * MSG, LANE))
        moe = jnp.concatenate([tall[l * TOK : (l + 1) * TOK] for l in range(TILES)], axis=1)
        mixed = res_v[...] + moe
        low, high = mixed[:, :width].astype(BF), mixed[:, width:].astype(BF)
        fin_v[...] = jnp.where(core == 0, high, low)
        put(fin_v, out_ref, one_send.at[FIN], one_recv.at[FIN], c, sib)
        out_ref[...] = jnp.where(core == 0, low, high)

    later(fin_v, one_send.at[FIN], active)
    later(out_ref, one_recv.at[FIN], idle)
    finish()


def local(C, NT, tokens, *args):
    (queries, key_rows, value_rows, out_gate, decay_index, w_out, norm_gain,
     expert_ids, gate_codes, w_gate, w_up, w_down) = args
    NZ = NT // 2
    H = NZ // 2
    E = C // 2
    PR = 2 * HEAD // E
    RQ = -(-E * CAP // 16) * 16
    D = NZ * SLAB
    vmem = pl.BlockSpec(memory_space=pltpu.VMEM)
    hbm = pl.BlockSpec(memory_space=pltpu.HBM)
    dma = pltpu.SemaphoreType.DMA
    return pl.pallas_call(
        functools.partial(kernel, C, NT, tokens),
        out_shape=jax.ShapeDtypeStruct((TOK, SLAB // 2), BF),
        in_specs=[pl.BlockSpec(memory_space=pltpu.SMEM)] + [hbm] * 11,
        out_specs=vmem,
        scratch_shapes=[
            pltpu.VMEM((TOK, 2 * HEAD), BF),
            pltpu.VMEM((TOK, 2 * HEAD), BF),
            pltpu.VMEM((TOK, 2 * HEAD), BF),
            pltpu.VMEM((TOK, 2 * HEAD), BF),
            pltpu.VMEM((D,), F32),
            pltpu.VMEM((TOP, TOK), jnp.int32),
            pltpu.VMEM((TOP, TOK), jnp.int32),
            pltpu.VMEM((2, 2 * HEAD, D), BF),
            pltpu.VMEM((4 * UNITS, D), BF),
            pltpu.VMEM((2 * UNITS, D), BF),
            pltpu.VMEM((E, PR, HEAD), BF),
            pltpu.VMEM((C, PR, HEAD), BF),
            pltpu.VMEM((C, PR, HEAD), BF),
            pltpu.VMEM((E, PR, HEAD), BF),
            pltpu.VMEM((TOK, 2 * HEAD), F32),
            pltpu.VMEM((TOK, 2 * HEAD), F32),
            pltpu.VMEM((TOK, 2 * HEAD), F32),
            pltpu.VMEM((TOK, 2 * HEAD), BF),
            pltpu.VMEM((TOK, 2 * HEAD), BF),
            pltpu.VMEM((NZ, TOK, WIDE), BF),
            pltpu.VMEM((NZ, TOK, SLAB), BF),
            pltpu.VMEM((E * MSG, TILES * TOK), BF),
            pltpu.VMEM((TILES * TOK, C * MSG), BF),
            pltpu.VMEM((TOK, SLAB), F32),
            pltpu.VMEM((E, MSG, LANE), BF),
            pltpu.VMEM((E, MSG, LANE), BF),
            pltpu.VMEM((TILES * RQ, E * MSG), BF),
            pltpu.VMEM((TILES, E * MSG, RQ), BF),
            pltpu.VMEM((NZ, RQ, SLAB), BF),
            pltpu.VMEM((RQ, 4 * UNITS), F32),
            pltpu.VMEM((RQ, LANE), F32),
            pltpu.VMEM((RQ, 2 * UNITS), BF),
            pltpu.VMEM((RQ, SLAB), BF),
            pltpu.VMEM((2, H, RQ, SLAB), BF),
            pltpu.VMEM((2, H, RQ, SLAB), BF),
            pltpu.VMEM((E, MSG, LANE), BF),
            pltpu.VMEM((C, MSG, LANE), BF),
            pltpu.VMEM((TOK, SLAB // 2), BF),
            dma((7,)),
            dma((4,)),
            dma((4,)),
            dma((4,)),
            dma((8,)),
            dma((8,)),
            dma((PARTS,)),
            dma((2, H, PARTS)),
            dma((2, H, PARTS)),
            dma((2, H, PARTS)),
            dma((2, H, PARTS)),
        ],
        compiler_params=pltpu.CompilerParams(
            collective_id=0, has_side_effects=True, vmem_limit_bytes=60 * 2**20
        ),
        cost_estimate=pl.CostEstimate(
            flops=1_000_000_000, bytes_accessed=8_000_000, transcendentals=100_000
        ),
        name="layer",
    )(
        decay_index,
        queries,
        key_rows,
        value_rows,
        out_gate,
        norm_gain,
        expert_ids.T,
        gate_codes.T,
        w_out,
        w_gate.transpose(0, 2, 1),
        w_up.transpose(0, 2, 1),
        w_down,
    )


def solution(mesh):
    C, NT = mesh.shape["ctx"], mesh.shape["tp"]
    placed = (
        P("ctx", "tp"),
        P("ctx", "tp"),
        P("ctx", "tp"),
        P("ctx", "tp"),
        P("tp"),
        P("tp", None),
        P(),
        P("ctx", None),
        P("ctx", None),
        P("ctx", None, "tp"),
        P("ctx", None, "tp"),
        P("ctx", "tp", None),
    )

    def whole(*args):
        tokens = args[0].shape[0]
        return jax.shard_map(
            functools.partial(local, C, NT, tokens),
            mesh=mesh,
            in_specs=placed,
            out_specs=P("ctx", "tp"),
            check_vma=False,
        )(*args)

    return whole
```

```python
import functools

import jax
import jax.numpy as jnp
from jax import lax
from jax.experimental import pallas as pl
from jax.experimental.pallas import tpu as pltpu
from jax.sharding import PartitionSpec as P

HEAD = 128
TOP = 2
NLEV = 16
CAP = 9
TOK = 64
SLAB = 384
LANE = 128
TILES = SLAB // LANE
MSG = 32
UNITS = 144
WIDE = 256
PARTS = 3
NX = 4
MESH = pl.DeviceIdType.MESH
BF = jnp.bfloat16
F32 = jnp.float32


def mm(a, b):
    return jnp.dot(a, b, preferred_element_type=F32)


def mm_t(a, b):
    return lax.dot_general(a, b, (((0,), (0,)), ((), ())), preferred_element_type=F32)


def mm_nt(a, b):
    return lax.dot_general(a, b, (((1,), (1,)), ((), ())), preferred_element_type=F32)


def wait_bytes(ref, sem):
    pltpu.make_async_copy(ref, ref, sem).wait()


def iota(shape, dim):
    return lax.broadcasted_iota(jnp.int32, shape, dim)


def kernel(
    C,
    NT,
    TOKENS,
    idx_ref,
    q_hbm,
    k_hbm,
    v_hbm,
    og_hbm,
    gain_hbm,
    ids_hbm,
    codes_hbm,
    wout_hbm,
    wg_hbm,
    wu_hbm,
    wd_hbm,
    out_ref,
    q_ref,
    k_ref,
    v_ref,
    og_ref,
    gain_ref,
    ids_ref,
    codes_ref,
    wout_v,
    w1_v,
    wd_v,
    state_v,
    win_v,
    pst_v,
    prior_v,
    open_v,
    inside_v,
    enter_v,
    ho_v,
    hs_v,
    rst_v,
    rsb_v,
    pick_v,
    comb_v,
    res_v,
    mst_v,
    arr_v,
    spread_v,
    gather_v,
    x_v,
    sum_v,
    square_v,
    hidden_v,
    last_v,
    sp_v,
    rp_v,
    m2_v,
    ret_v,
    fin_v,
    in_sem,
    wl_sem,
    ws_sem,
    wr_sem,
    one_send,
    one_recv,
    disp_recv,
    ag_send,
    ag_recv,
    rs_send,
    rs_recv,
):
    NZ = NT // 2
    H = NZ // 2
    E = C // 2
    PR = 2 * HEAD // E
    RQ = x_v.shape[1]
    D = NZ * SLAB
    NY = C // NX
    units = RQ // 16
    count = min(PARTS, units)
    edges = [16 * (units * p // count) for p in range(count + 1)]
    parts = [(a, b - a) for a, b in zip(edges, edges[1:])]
    split = (count + 1) // 2
    begins = [e // CAP for e in edges[:-1]]
    reach = [0] + [min(E, -(-e // CAP)) for e in edges[1:]]
    whole = [0] + [min(E, e // CAP) for e in edges[1:]]

    c = lax.axis_index("ctx")
    t = lax.axis_index("tp")
    z = lax.div(t, 2)
    core = lax.rem(t, 2)
    sib = t + 1 - 2 * core
    side = lax.rem(c, 2)
    mine = lax.div(c, 2)
    active = side == core
    idle = jnp.logical_not(active)
    y_at = lax.div(c, NX)
    x_at = lax.rem(c, NX)

    def falling(n):
        return sorted(range(n), key=lambda d: -min(d, n - d))

    def rank(d):
        return 0 if d == 0 else 2 * d - 1 if d <= NY // 2 else 2 * (NY - d)

    at_y = [lax.rem(y_at + d, NY) for d in range(NY)]
    at_x = [lax.rem(x_at + d, NX) for d in range(NX)]
    pair_x = [lax.div(x, 2) for x in at_x]
    slabs = [lax.rem(z + d, NZ) for d in range(NZ)]
    everyone = [(dy, dx) for dy in falling(NY) for dx in falling(NX)][:-1]

    def ctx_at(dy, dx):
        return NX * at_y[dy] + at_x[dx]

    own_slot = pair_x[0]

    ST1, ST2, HO, RS, PAIR, DISP, RETN, FIN = range(8)

    def put(src, dst, send, recv, ctx, tp):
        pltpu.make_async_remote_copy(
            src_ref=src,
            dst_ref=dst,
            send_sem=send,
            recv_sem=recv,
            device_id={"ctx": ctx, "tp": tp},
            device_id_type=MESH,
        ).start()

    drains = []

    def later(ref, sem, when=None):
        drains.append((ref, sem, when))

    def finish():
        for ref, sem, when in drains:
            if when is None:
                wait_bytes(ref, sem)
            else:
                pl.when(when)(functools.partial(wait_bytes, ref, sem))
        drains.clear()

    inputs = (
        (k_hbm, k_ref),
        (v_hbm, v_ref),
        (q_hbm, q_ref),
        (og_hbm, og_ref),
        (ids_hbm, ids_ref),
        (codes_hbm, codes_ref),
        (gain_hbm, gain_ref),
    )
    loads = [
        pltpu.make_async_copy(src, dst, in_sem.at[n]) for n, (src, dst) in enumerate(inputs)
    ]
    for load in loads:
        load.start()

    barrier = pltpu.get_barrier_semaphore()

    def greet(ctx, tp):
        pl.semaphore_signal(
            barrier, inc=1, device_id={"ctx": ctx, "tp": tp}, device_id_type=MESH
        )

    def beside(dz):
        return 2 * slabs[dz] + 1 - side

    ring_peers = sorted({1, 2 % NZ, NZ - 2, NZ - 1} - {0})

    for dy, dx in everyone:
        if dx % 2:
            greet(ctx_at(dy, dx), t)
    for dz in range(1, NZ):
        greet(c, 2 * slabs[dz] + side)

    @pl.when(active)
    def _():
        for dy, dx in everyone:
            if dx % 2 == 0:
                greet(ctx_at(dy, dx), t)
        for dz in range(NZ):
            greet(c, beside(dz))

    @pl.when(idle)
    def _():
        greet(c, sib)
        for dz in ring_peers:
            greet(c, beside(dz))

    def rows_of(ref, n):
        return ref.at[pl.ds(n * UNITS, UNITS)]

    weights = (
        (wout_hbm, wout_v.at[0], wout_v.at[1]),
        (wg_hbm.at[0], rows_of(w1_v, 0), rows_of(w1_v, 1)),
        (wu_hbm.at[0], rows_of(w1_v, 2), rows_of(w1_v, 3)),
        (wd_hbm.at[0], rows_of(wd_v, 0), rows_of(wd_v, 1)),
    )
    for n, (src, here, there) in enumerate(weights):
        pltpu.make_async_copy(src, here, wl_sem.at[n]).start()

    def have(n):
        src, here, there = weights[n]
        pltpu.make_async_copy(src, here, wl_sem.at[n]).wait()
        wait_bytes(there, wr_sem.at[n])

    log_fast = jnp.log(jnp.full((1, 1), 1.0 / 40.0, F32))
    log_slow = jnp.log(jnp.full((1, 1), 1.0 / (16.0 * TOKENS), F32))
    rates = []
    for h in range(2):
        fraction = jnp.full((1, 1), idx_ref[h].astype(F32), F32) / (NLEV - 1)
        rates.append(jnp.exp(log_fast + fraction * (log_slow - log_fast)))
    place = iota((TOK, 1), 0).astype(F32)
    loads[0].wait()
    loads[1].wait()
    for h in range(2):
        cols = slice(h * HEAD, (h + 1) * HEAD)
        fading = jnp.exp(-rates[h] * (TOK - 1.0 - place))
        faded = (k_ref[:, cols].astype(F32) * fading).astype(BF)
        state = mm_t(faded, v_ref[:, cols]).astype(BF)
        each = HEAD // PR
        state_v[h * each : (h + 1) * each] = state.reshape(each, PR, HEAD)

    @pl.when(active)
    def _():
        pl.semaphore_wait(barrier, C - 1 + NT - 1)

    @pl.when(idle)
    def _():
        pl.semaphore_wait(barrier, E + NZ + len(ring_peers))

    def to_pair(dy, k):
        half = lax.rem(own_slot + k, NX // 2)
        j = NX // 2 * at_y[dy] + half
        return j, 2 * j + core

    far_pairs = [(dy, k) for dy in falling(NY) for k in falling(NX // 2)]

    def send_piece(dy, k):
        j, to = to_pair(dy, k)
        put(state_v.at[j], win_v.at[c], one_send.at[ST1], one_recv.at[ST1], to, t)

    for dy, k in far_pairs[:-1]:
        send_piece(dy, k)

    @pl.when(idle)
    def _():
        send_piece(0, 0)

    later(state_v.at[pl.ds(0, E - 1)], one_send.at[ST1], active)
    later(state_v, one_send.at[ST1], idle)
    for n, (src, here, there) in enumerate(weights):
        put(src, there, ws_sem.at[n], wr_sem.at[n], c, sib)
        later(there, ws_sem.at[n])

    for load in loads[2:]:
        load.wait()
    n_at, m_at = iota((TOK, TOK), 0), iota((TOK, TOK), 1)
    offsets = (n_at - m_at).astype(F32)
    for h in range(2):
        cols = slice(h * HEAD, (h + 1) * HEAD)
        scores = mm_nt(q_ref[:, cols], k_ref[:, cols])
        within = jnp.where(
            offsets >= 0.0, jnp.exp(-rates[h] * jnp.maximum(offsets, 0.0)), 0.0
        )
        inside_v[:, cols] = mm((scores * within).astype(BF), v_ref[:, cols])
    open_v[...] = jax.nn.sigmoid(og_ref[...].astype(F32))
    enter_v[...] = jnp.concatenate(
        [
            jnp.broadcast_to(jnp.exp(-rates[h] * (place + 1.0)), (TOK, HEAD))
            for h in range(2)
        ],
        axis=1,
    )

    @pl.when(active)
    def _():
        win_v[c] = state_v[mine]
        wait_bytes(win_v.at[pl.ds(0, C - 1)], one_recv.at[ST1])
        first_head = mine * PR < HEAD
        decay = jnp.exp(-jnp.where(first_head, rates[0], rates[1]) * TOK)

        def turn(b, run):
            pst_v[b] = run.astype(BF)
            return run * decay + win_v[b].astype(F32)

        lax.fori_loop(0, C, turn, jnp.zeros((PR, HEAD), F32), unroll=True)

        for dy, dx in everyone:
            to = ctx_at(dy, dx)
            put(pst_v.at[to], prior_v.at[mine], one_send.at[ST2], one_recv.at[ST2], to, t)
        prior_v[mine] = pst_v[c]

    later(pst_v.at[pl.ds(0, C - 1)], one_send.at[ST2], active)

    @pl.when(active)
    def _():
        eye = n_at == m_at

        def stand(row):
            return jnp.sum(jnp.where(eye, row, 0.0), axis=1, keepdims=True)

        def lie(column):
            return jnp.sum(jnp.where(eye, column, 0.0), axis=0, keepdims=True)

        ids = [stand(ids_ref[j : j + 1].astype(F32)) for j in range(TOP)]
        codes = [codes_ref[j : j + 1].astype(F32) for j in range(TOP)]
        share = [stand(codes[j] / (codes[0] + codes[1])) for j in range(TOP)]
        expert_at = iota((TOK, LANE), 1).astype(F32)
        hot = [jnp.where(expert_at == ids[j], 1.0, 0.0) for j in range(TOP)]
        before = jnp.where(n_at > m_at, 1.0, 0.0).astype(BF)
        ahead = mm(before, (hot[0] + hot[1]).astype(BF))
        rank = [jnp.sum(hot[j] * ahead, axis=1, keepdims=True) for j in range(TOP)]
        out_row = [lie(MSG * ids[j] + rank[j]) for j in range(TOP)]
        back_row = [2 * MSG * ids[j] + rank[j] for j in range(TOP)]
        row_at = iota((E * MSG, TOK), 0).astype(F32)
        both_at = iota((TOK, C * MSG), 1)
        both_at = (both_at - MSG * lax.rem(lax.div(both_at, MSG), 2)).astype(F32)
        for l in range(TILES):
            taken = (row_at == out_row[0] + CAP * l) | (row_at == out_row[1] + CAP * l)
            pick_v[:, l * TOK : (l + 1) * TOK] = jnp.where(taken, 1.0, 0.0).astype(BF)
            comb_v[l * TOK : (l + 1) * TOK] = (
                jnp.where(both_at == back_row[0] + CAP * l, share[0], 0.0)
                + jnp.where(both_at == back_row[1] + CAP * l, share[1], 0.0)
            ).astype(BF)

    for p, (begin, size) in enumerate(parts):
        deep = MSG * (reach[p + 1] - begins[p])
        if deep:
            row, at = begin + iota((size, deep), 0), iota((size, deep), 1)
            row = MSG * (lax.div(row, CAP) - begins[p]) + lax.rem(row, CAP)
            for l in range(TILES):
                start = TILES * begin + l * size
                spread_v[start : start + size, :deep] = jnp.where(
                    at == row + CAP * l, 1.0, 0.0
                ).astype(BF)
        low, high = whole[p], whole[p + 1]
        if low < high:
            base = CAP * low // 16 * 16
            shape = (MSG * (high - low), edges[p + 1] - base)
            at, row = MSG * low + iota(shape, 0), base + iota(shape, 1)
            row = MSG * lax.div(row, CAP) + lax.rem(row, CAP)
            for l in range(TILES):
                gather_v[l, MSG * low : MSG * high, : shape[1]] = jnp.where(
                    at == row + CAP * l, 1.0, 0.0
                ).astype(BF)

    pl.when(active)(
        functools.partial(wait_bytes, prior_v.at[pl.ds(0, E - 1)], one_recv.at[ST2])
    )
    pl.when(idle)(functools.partial(wait_bytes, prior_v, one_recv.at[ST2]))
    prior = prior_v[...].reshape(2 * HEAD, HEAD)
    for h in range(2):
        cols = slice(h * HEAD, (h + 1) * HEAD)
        outside = mm(q_ref[:, cols], prior[h * HEAD : (h + 1) * HEAD])
        attended = inside_v[:, cols] + outside * enter_v[:, cols]
        scale = lax.rsqrt(jnp.mean(attended * attended, axis=1, keepdims=True) + 1e-06)
        ho_v[:, cols] = (attended * scale * open_v[:, cols]).astype(BF)

    put(ho_v, hs_v, one_send.at[HO], one_recv.at[HO], c, sib)
    later(hs_v, one_send.at[HO])
    have(0)
    wait_bytes(hs_v, one_recv.at[HO])

    lead = 2 * z + side
    order = sorted(range(NZ), key=lambda i: -min(i, NZ - i))

    def project(begin, size):
        lanes = pl.ds(begin, size)
        for i in order:
            zz = slabs[i]
            cols = pl.ds(pl.multiple_of(zz * SLAB, SLAB) + begin, size)
            part = mm(ho_v[...], wout_v[0, :, cols]) + mm(hs_v[...], wout_v[1, :, cols])
            rst_v[i, :, :size] = part.astype(BF)
            if i:
                put(
                    rst_v.at[i, :, pl.ds(0, size)],
                    rsb_v.at[z, :, lanes],
                    one_send.at[RS],
                    one_recv.at[RS],
                    c,
                    2 * zz + side,
                )

        @pl.when(idle)
        def _():
            put(
                rst_v.at[0, :, pl.ds(0, size)],
                rsb_v.at[z, :, lanes],
                one_send.at[PAIR],
                one_recv.at[PAIR],
                c,
                lead,
            )

        @pl.when(active)
        def _():
            rsb_v[z, :, begin : begin + size] = rst_v[0, :, :size]

    for k, (begin, size) in enumerate(((0, WIDE), (WIDE, SLAB - WIDE))):
        here = core == k
        pl.when(here)(functools.partial(project, begin, size))
        later(rst_v.at[pl.ds(0, NZ - 1), :, pl.ds(0, size)], one_send.at[RS], here)
        later(rst_v.at[0, :, pl.ds(0, size)], one_send.at[PAIR], here & idle)

    @pl.when(active)
    def _():
        for k, size in enumerate((SLAB - WIDE, WIDE)):
            pl.when(core == k)(
                functools.partial(
                    wait_bytes, rsb_v.at[0, :, pl.ds(0, size)], one_recv.at[PAIR]
                )
            )
        wait_bytes(rsb_v.at[pl.ds(0, NZ - 1)], one_recv.at[RS])
        gain = gain_ref[pl.ds(pl.multiple_of(z * SLAB, SLAB), SLAB)].reshape(1, SLAB)
        total = rsb_v[0].astype(F32)
        for zz in range(1, NZ):
            total = total + rsb_v[zz].astype(F32)
        res_v[...] = total
        scaled = (total * gain).astype(BF)
        stacked = jnp.concatenate(
            [scaled[:, l * LANE : (l + 1) * LANE] for l in range(TILES)], axis=0
        )
        mst_v[...] = mm(pick_v[...], stacked).astype(BF).reshape(E, MSG, LANE)

        for dy, dx in everyone:
            first = NX // 2 * rank((NY - dy) % NY)
            groups = [sum(first + k >= r for r in reach[1:-1]) for k in range(NX // 2)]
            group = groups[0]
            for k in range(1, NX // 2):
                group = group + (groups[k] - groups[k - 1]) * lax.div(own_slot, k)
            put(
                mst_v.at[NX // 2 * at_y[dy] + pair_x[dx]],
                arr_v.at[first + own_slot],
                one_send.at[DISP],
                disp_recv.at[group],
                ctx_at(dy, dx),
                t,
            )
        arr_v[own_slot] = mst_v[mine]

    for _ in range(2):
        later(mst_v.at[pl.ds(0, E - 1)], one_send.at[DISP], active)
    later(mst_v.at[0], one_send.at[DISP], active)

    def at_z(step):
        return slabs[step % NZ]

    def carried(step, way):
        if step < H:
            return range(count)
        return range(split) if way == 0 else range(split, count)

    def pass_on(step, hops, way, n, p):
        turn = 1 - 2 * way
        begin, size = parts[p]
        piece = x_v.at[at_z(step), pl.ds(begin, size)]
        put(
            piece,
            piece,
            ag_send.at[way, n, p],
            ag_recv.at[way, n, p],
            c,
            2 * at_z(turn * hops) + core,
        )
        later(piece, ag_send.at[way, n, p])

    def landed(step, way, n, p):
        begin, size = parts[p]
        wait_bytes(x_v.at[at_z(step), pl.ds(begin, size)], ag_recv.at[way, n, p])

    def take(step, p=None):
        chunk = at_z(step)
        cols = pl.ds(pl.multiple_of(chunk * SLAB, SLAB), SLAB)
        begin, size = (0, RQ) if p is None else parts[p]
        rows = pl.ds(begin, size)
        x = x_v[chunk, rows]
        new = mm_nt(x, w1_v[:, cols])
        wide = x.astype(F32) * (1.0 / gain_ref[cols].reshape(1, SLAB))
        wide = wide * wide
        squares = wide[:, :LANE]
        for l in range(1, TILES):
            squares = squares + wide[:, l * LANE : (l + 1) * LANE]
        if step == 0:
            sum_v[rows] = new
            square_v[rows] = squares
        elif p is None:
            sum_v[rows] += new
            square_v[rows] += squares
        else:
            return sum_v[rows] + new, square_v[rows] + squares

    def down(step, hidden):
        cols = pl.ds(pl.multiple_of(at_z(step) * SLAB, SLAB), SLAB)
        return mm(hidden, wd_v[:, cols])

    def add_up(step, way, p, value):
        begin, size = parts[p]
        piece = pl.ds(begin, size)
        sp_v[way, step - 1, piece] = value.astype(BF)
        put(
            sp_v.at[way, step - 1, piece],
            rp_v.at[way, step - 1, piece],
            rs_send.at[way, step - 1, p],
            rs_recv.at[way, step - 1, p],
            c,
            2 * at_z(1 - 2 * way) + core,
        )
        later(sp_v.at[way, step - 1, piece], rs_send.at[way, step - 1, p])

    for p, (begin, size) in enumerate(parts):
        low, high = reach[p], reach[p + 1]
        if low < high:
            if p == 0:
                pl.when(active)(
                    functools.partial(
                        wait_bytes, arr_v.at[pl.ds(0, high - 1)], disp_recv.at[0]
                    )
                )
                pl.when(idle)(
                    functools.partial(wait_bytes, arr_v.at[pl.ds(0, high)], disp_recv.at[0])
                )
            else:
                wait_bytes(arr_v.at[pl.ds(low, high - low)], disp_recv.at[p])
        deep = MSG * (high - begins[p])
        if deep:
            rows = arr_v[begins[p] : high].reshape(deep, LANE)
            start = TILES * begin
            spread = mm(spread_v[start : start + TILES * size, :deep], rows).astype(BF)
            for l in range(TILES):
                x_v[z, begin : begin + size, l * LANE : (l + 1) * LANE] = spread[
                    l * size : (l + 1) * size
                ]
        else:
            x_v[z, begin : begin + size] = jnp.zeros((size, SLAB), BF)
        for hops in (2, 1) if H == 4 else (1,):
            for way in range(2):
                if p in carried(hops, way):
                    pass_on(0, hops, way, hops - 1, p)
    have(1)
    have(2)
    ready = [0]
    if H == 4:
        for p in range(count):
            for way in range(2):
                back = 4 * way - 2
                landed(back, way, 1, p)
                if p in carried(H, way):
                    pass_on(back, 2, way, 3, p)
                pass_on(back, 1, way, 2, p)
        take(0)
        for n in (0, 1, 2):
            if n != 1:
                for p in range(count):
                    for way in range(2):
                        landed((2 * way - 1) * (n + 1), way, n, p)
            take(n + 1)
            take(-n - 1)
    else:
        for step in range(1, H):
            for p in range(count):
                for way in range(2):
                    landed((2 * way - 1) * step, way, step - 1, p)
                    if p in carried(step + 1, way):
                        pass_on((2 * way - 1) * step, 1, way, step, p)
            while ready:
                take(ready.pop(0))
            ready = [-step, step]
        while ready:
            take(ready.pop(0))
    have(3)

    for p in sorted(range(count), key=lambda p: p if p < split else p - split + 0.5):
        way = 0 if p < split else 1
        begin, size = parts[p]
        wait_bytes(x_v.at[at_z(H), pl.ds(begin, size)], ag_recv.at[way, H - 1, p])
        sums, squares = take(H, p)
        inverse = lax.rsqrt(jnp.sum(squares, axis=1, keepdims=True) / D + 1e-05)
        gate = sums[:, : 2 * UNITS] * inverse
        up = sums[:, 2 * UNITS :] * inverse
        hidden = (jax.nn.silu(gate) * up).astype(BF)
        hidden_v[begin : begin + size] = hidden
        add_up(1, way, p, down(H, hidden))

    for step in range(2, H + 1):
        values = (down(H + 1 - step, hidden_v[...]), down(step - H - 1, hidden_v[...]))
        for p in range(count):
            begin, size = parts[p]
            piece = pl.ds(begin, size)
            for way in range(2):
                value = values[way][begin : begin + size]
                if step > 2 or p in carried(H, way):
                    wait_bytes(rp_v.at[way, step - 2, piece], rs_recv.at[way, step - 2, p])
                    value = value + rp_v[way, step - 2, piece].astype(F32)
                add_up(step, way, p, value)

    own = down(0, hidden_v[...])

    by_rank = sorted(range(NY), key=rank)

    def send_back(slot):
        dy, k = by_rank[slot // (NX // 2)], slot % (NX // 2)
        to = NX * at_y[dy] + 2 * k + core

        def go():
            put(m2_v.at[slot], ret_v.at[c], one_send.at[RETN], one_recv.at[RETN], to, t)

        if dy:
            go()
        else:
            pl.when(jnp.logical_not(active & (own_slot == k)))(go)

    for p, (begin, size) in enumerate(parts):
        piece = pl.ds(begin, size)
        value = own[begin : begin + size]
        for way in range(2):
            if H > 1 or p in carried(H, way):
                wait_bytes(rp_v.at[way, H - 1, piece], rs_recv.at[way, H - 1, p])
                value = value + rp_v[way, H - 1, piece].astype(F32)
        last_v[piece] = value.astype(BF)
        low, high = whole[p], whole[p + 1]
        if low < high:
            base = CAP * low // 16 * 16
            deep = edges[p + 1] - base
            message = jnp.zeros((MSG * (high - low), LANE), F32)
            for l in range(TILES):
                message = message + mm(
                    gather_v[l, MSG * low : MSG * high, :deep],
                    last_v[base : base + deep, l * LANE : (l + 1) * LANE],
                )
            m2_v[low:high] = message.astype(BF).reshape(high - low, MSG, LANE)
            for slot in reversed(range(low, high)):
                send_back(slot)
    finish()
    later(m2_v.at[pl.ds(0, E - 1)], one_send.at[RETN], active)
    later(m2_v, one_send.at[RETN], idle)
    width = out_ref.shape[1]

    @pl.when(active)
    def _():
        ret_v[c] = m2_v[own_slot]
        wait_bytes(ret_v.at[pl.ds(0, C - 1)], one_recv.at[RETN])
        tall = mm(comb_v[...], ret_v[...].reshape(C * MSG, LANE))
        moe = jnp.concatenate([tall[l * TOK : (l + 1) * TOK] for l in range(TILES)], axis=1)
        mixed = res_v[...] + moe
        low, high = mixed[:, :width].astype(BF), mixed[:, width:].astype(BF)
        fin_v[...] = jnp.where(core == 0, high, low)
        put(fin_v, out_ref, one_send.at[FIN], one_recv.at[FIN], c, sib)
        out_ref[...] = jnp.where(core == 0, low, high)

    later(fin_v, one_send.at[FIN], active)
    later(out_ref, one_recv.at[FIN], idle)
    finish()


def local(C, NT, tokens, *args):
    (queries, key_rows, value_rows, out_gate, decay_index, w_out, norm_gain,
     expert_ids, gate_codes, w_gate, w_up, w_down) = args
    NZ = NT // 2
    H = NZ // 2
    E = C // 2
    PR = 2 * HEAD // E
    RQ = -(-E * CAP // 16) * 16
    D = NZ * SLAB
    vmem = pl.BlockSpec(memory_space=pltpu.VMEM)
    hbm = pl.BlockSpec(memory_space=pltpu.HBM)
    dma = pltpu.SemaphoreType.DMA
    return pl.pallas_call(
        functools.partial(kernel, C, NT, tokens),
        out_shape=jax.ShapeDtypeStruct((TOK, SLAB // 2), BF),
        in_specs=[pl.BlockSpec(memory_space=pltpu.SMEM)] + [hbm] * 11,
        out_specs=vmem,
        scratch_shapes=[
            pltpu.VMEM((TOK, 2 * HEAD), BF),
            pltpu.VMEM((TOK, 2 * HEAD), BF),
            pltpu.VMEM((TOK, 2 * HEAD), BF),
            pltpu.VMEM((TOK, 2 * HEAD), BF),
            pltpu.VMEM((D,), F32),
            pltpu.VMEM((TOP, TOK), jnp.int32),
            pltpu.VMEM((TOP, TOK), jnp.int32),
            pltpu.VMEM((2, 2 * HEAD, D), BF),
            pltpu.VMEM((4 * UNITS, D), BF),
            pltpu.VMEM((2 * UNITS, D), BF),
            pltpu.VMEM((E, PR, HEAD), BF),
            pltpu.VMEM((C, PR, HEAD), BF),
            pltpu.VMEM((C, PR, HEAD), BF),
            pltpu.VMEM((E, PR, HEAD), BF),
            pltpu.VMEM((TOK, 2 * HEAD), F32),
            pltpu.VMEM((TOK, 2 * HEAD), F32),
            pltpu.VMEM((TOK, 2 * HEAD), F32),
            pltpu.VMEM((TOK, 2 * HEAD), BF),
            pltpu.VMEM((TOK, 2 * HEAD), BF),
            pltpu.VMEM((NZ, TOK, WIDE), BF),
            pltpu.VMEM((NZ, TOK, SLAB), BF),
            pltpu.VMEM((E * MSG, TILES * TOK), BF),
            pltpu.VMEM((TILES * TOK, C * MSG), BF),
            pltpu.VMEM((TOK, SLAB), F32),
            pltpu.VMEM((E, MSG, LANE), BF),
            pltpu.VMEM((E, MSG, LANE), BF),
            pltpu.VMEM((TILES * RQ, E * MSG), BF),
            pltpu.VMEM((TILES, E * MSG, RQ), BF),
            pltpu.VMEM((NZ, RQ, SLAB), BF),
            pltpu.VMEM((RQ, 4 * UNITS), F32),
            pltpu.VMEM((RQ, LANE), F32),
            pltpu.VMEM((RQ, 2 * UNITS), BF),
            pltpu.VMEM((RQ, SLAB), BF),
            pltpu.VMEM((2, H, RQ, SLAB), BF),
            pltpu.VMEM((2, H, RQ, SLAB), BF),
            pltpu.VMEM((E, MSG, LANE), BF),
            pltpu.VMEM((C, MSG, LANE), BF),
            pltpu.VMEM((TOK, SLAB // 2), BF),
            dma((7,)),
            dma((4,)),
            dma((4,)),
            dma((4,)),
            dma((8,)),
            dma((8,)),
            dma((PARTS,)),
            dma((2, H, PARTS)),
            dma((2, H, PARTS)),
            dma((2, H, PARTS)),
            dma((2, H, PARTS)),
        ],
        compiler_params=pltpu.CompilerParams(
            collective_id=0, has_side_effects=True, vmem_limit_bytes=60 * 2**20
        ),
        cost_estimate=pl.CostEstimate(
            flops=1_000_000_000, bytes_accessed=8_000_000, transcendentals=100_000
        ),
        name="layer",
    )(
        decay_index,
        queries,
        key_rows,
        value_rows,
        out_gate,
        norm_gain,
        expert_ids.T,
        gate_codes.T,
        w_out,
        w_gate.transpose(0, 2, 1),
        w_up.transpose(0, 2, 1),
        w_down,
    )


def solution(mesh):
    C, NT = mesh.shape["ctx"], mesh.shape["tp"]
    placed = (
        P("ctx", "tp"),
        P("ctx", "tp"),
        P("ctx", "tp"),
        P("ctx", "tp"),
        P("tp"),
        P("tp", None),
        P(),
        P("ctx", None),
        P("ctx", None),
        P("ctx", None, "tp"),
        P("ctx", None, "tp"),
        P("ctx", "tp", None),
    )

    def whole(*args):
        tokens = args[0].shape[0]
        return jax.shard_map(
            functools.partial(local, C, NT, tokens),
            mesh=mesh,
            in_specs=placed,
            out_specs=P("ctx", "tp"),
            check_vma=False,
        )(*args)

    return whole
```
